32 devices in a mesh: blk: 8 (over z, y), rank: 4 (over x, core).
Axes of the slice: x: 2, y: 2, z: 4, core: 2. Of those that a mesh axis runs over, the one named last changes fastest.
Arguments:
- user_factors: float32 [256, 4096], P('rank', 'blk'), may hold values from -1.5 to 1.5
- item_factors: float32 [256, 8192], P('rank', 'blk'), may hold values from -1.5 to 1.5
- tile_rows: int32 [8, 4, 4096], P('blk'), may hold values from 0 to 511
- tile_cols: int32 [8, 4, 4096], P('blk'), may hold values from 0 to 1023
- tile_vals: float32 [8, 4, 4096], P('blk'), may hold values from -4 to 4
- tile_count: int32 [8, 4], P('blk'), may hold values from 512 to 4096, as said below
Outputs:
- new_users: float32 [256, 4096], P('rank', 'blk')
- new_items: float32 [256, 8192], P('rank', 'blk')
The draws below stay inside these ranges and needn't reach their ends.
Inputs may be any that keep to these rules, and one draw needn't show every extreme that they name: `tile_count`: in every stratum some block's tile is full (4096 live slots).
All inputs are finite; a program needn't handle non-finite values.
Results may differ from the reference program's by a relative error of at most 0.0003.
Values sent between devices are 32-bit elements; how exact they have to be, the bound alone decides.
A program may use at most 64 MiB of HBM per device.

```python
import jax
import jax.numpy as jnp
from jax import lax

R = 256
USERS_DEV = 512
ITEMS_DEV = 1024
TILE = 4096
BATCH = 1024
STRATA = 4
BLOCKS = 8
USERS = 4096
ITEMS = 8192


def draw_tile_count(key, part):
    key_counts, key_pick = jax.random.split(key)
    counts = jax.random.randint(key_counts, (BLOCKS, STRATA), TILE // 8, TILE + 1, dtype=jnp.int32)
    chosen = jax.random.randint(key_pick, (1, STRATA), 0, BLOCKS, dtype=jnp.int32)
    block_ids = jnp.arange(BLOCKS, dtype=jnp.int32)[:, None]
    return jnp.where(block_ids == chosen, TILE, counts).astype(jnp.int32)


def touch_ends(drawn, rng, low, top_value):
    dims = drawn.shape
    place = [jax.random.randint(jax.random.fold_in(rng, axis), (), 0, dims[axis]) for axis in range(len(dims))]
    drawn = drawn.at[tuple(place)].set(low)
    longest = dims.index(max(dims))
    place[longest] = (place[longest] + 1) % dims[longest]
    return drawn.at[tuple(place)].set(top_value)


def block_levels(own_key, extent, cuts, smallest, largest):
    gain, own = 1.0, jax.random.fold_in(own_key, 6)
    for axis_at, shards_of in cuts:
        heights = jnp.exp(jax.random.uniform(jax.random.fold_in(own, axis_at), (shards_of,), jnp.float32, smallest / len(cuts), largest / len(cuts)))
        gain = gain * jnp.repeat(heights, extent[axis_at] // shards_of).reshape([-1 if axis == axis_at else 1 for axis in range(len(extent))])
    return gain


def bell_draw(stream_key, extent, deviation, limit, cuts=(), kind=jnp.bfloat16):
    gain = block_levels(stream_key, extent, cuts, -0.22, 0.18) if cuts else 1.0
    values = jax.random.normal(stream_key, extent, jnp.float32) * deviation * gain
    return jnp.minimum(jnp.maximum(values, -limit), limit).astype(kind)


def setup_inputs(seed: int = 0) -> dict:
    key_list = jax.random.split(jax.random.key(seed), 7)
    return {
        "user_factors": bell_draw(key_list[0], (R, USERS), 0.25, 1.5, ((0, 4), (1, 8)), jnp.float32),
        "item_factors": bell_draw(key_list[1], (R, ITEMS), 0.25, 1.5, ((0, 4), (1, 8)), jnp.float32),
        "tile_rows": touch_ends(jax.random.randint(key_list[2], (BLOCKS, STRATA, TILE), 0, USERS_DEV), jax.random.fold_in(key_list[2], 1), 0, USERS_DEV - 1).astype(jnp.int32),
        "tile_cols": touch_ends(jax.random.randint(key_list[3], (BLOCKS, STRATA, TILE), 0, ITEMS_DEV), jax.random.fold_in(key_list[3], 1), 0, ITEMS_DEV - 1).astype(jnp.int32),
        "tile_vals": bell_draw(key_list[4], (BLOCKS, STRATA, TILE), 1.0, 4.0, ((0, 8),), jnp.float32),
        "tile_count": draw_tile_count(jax.random.fold_in(key_list[6], 71), 0),
    }


LEARN_RATE = 0.05
DECAY_WEIGHT = 0.02


def sweep_tile(user_block, item_block, row_index, col_index, rating_vals, live_count):
    def update(batch_index, carry):
        user_now, item_now = carry
        offset = (batch_index * BATCH).astype(jnp.int32)
        user_rows = lax.dynamic_slice_in_dim(row_index, offset, BATCH)
        item_rows = lax.dynamic_slice_in_dim(col_index, offset, BATCH)
        targets = lax.dynamic_slice_in_dim(rating_vals, offset, BATCH)
        positions = offset + jnp.arange(BATCH, dtype=jnp.int32)
        weights = (positions < live_count).astype(jnp.float32)
        user_vecs = user_now[user_rows]
        item_vecs = item_now[item_rows]
        predicted = jnp.sum(user_vecs * item_vecs, axis=1)
        errors = weights * (targets - predicted)
        user_step = LEARN_RATE * (errors[:, None] * item_vecs - DECAY_WEIGHT * weights[:, None] * user_vecs)
        item_step = LEARN_RATE * (errors[:, None] * user_vecs - DECAY_WEIGHT * weights[:, None] * item_vecs)
        return user_now.at[user_rows].add(user_step), item_now.at[item_rows].add(item_step)

    return lax.fori_loop(0, TILE // BATCH, update, (user_block, item_block))


def reference(user_factors, item_factors, tile_rows, tile_cols, tile_vals, tile_count):
    user_blocks = user_factors.T.reshape(BLOCKS, USERS_DEV, R)
    item_blocks = item_factors.T.reshape(BLOCKS, ITEMS_DEV, R)
    for stratum in range(STRATA):
        turned = jnp.roll(item_blocks, stratum, axis=0)
        user_blocks, turned = jax.vmap(sweep_tile)(user_blocks, turned, tile_rows[:, stratum], tile_cols[:, stratum], tile_vals[:, stratum], tile_count[:, stratum])
        item_blocks = jnp.roll(turned, -stratum, axis=0)
    return user_blocks.reshape(USERS, R).T, item_blocks.reshape(ITEMS, R).T
```

```python
import functools

import jax
import jax.numpy as jnp
from jax import lax
from jax.experimental import pallas as pl
from jax.experimental.pallas import tpu as pltpu
from jax.sharding import PartitionSpec as P

BATCH = 1024
LANES = 128
GROUPS = BATCH // LANES
CHUNK = 256
PACK = 16
LEARN_RATE = 0.05
DECAY_WEIGHT = 0.02
MESH = pl.DeviceIdType.MESH


def split_rows(block):
    high = block.astype(jnp.bfloat16)
    low = (block - high.astype(jnp.float32)).astype(jnp.bfloat16)
    return high, low


def kernel(
    blocks, ranks,
    u_in, v_in, rows_in, cols_in, vals_in, count_in,
    u_out, v_out,
    rows, cols, vals, count, users, u_cat, v_cat, held, tiles, chooser, spreader, u_pick, v_pick, u_step, v_step,
    partial, arrived, errs,
    part_send, part_recv, tile_send, tile_recv, user_send, user_recv, load_sem,
):
    depth, user_count = u_in.shape
    item_count = v_in.shape[1]
    strata, tile = rows_in.shape[1:]
    per_tile = tile // BATCH
    spans = tile // LANES
    blk = lax.axis_index("blk")
    rank = lax.axis_index("rank")

    def at_blk(shift):
        return (lax.rem(blk + (shift % blocks), blocks), rank)

    def at_rank(shift):
        return (blk, lax.rem(rank + (shift % ranks), ranks))

    barrier = pltpu.get_barrier_semaphore()
    met = [at_rank(o) for o in range(1, ranks)]
    met += [at_blk(o) for o in range(1, strata)] + [at_blk(-o) for o in range(1, strata)]
    for device in met:
        pl.semaphore_signal(barrier, inc=1, device_id=device, device_id_type=MESH)

    loads = [
        pltpu.make_async_copy(source, target, load_sem.at[i])
        for i, (source, target) in enumerate(
            (
                (count_in, count), (rows_in, rows), (cols_in, cols), (vals_in, vals),
                (u_in, users.at[0]), (v_in, v_out),
            )
        )
    ]
    for load in loads:
        load.start()
    for load in loads[:3]:
        load.wait()

    stratum_at = lax.broadcasted_iota(jnp.int32, (strata, LANES), 0)
    lane_at = lax.broadcasted_iota(jnp.int32, (strata, LANES), 1)
    live = jnp.zeros((strata, LANES), jnp.int32)
    for s in range(strata):
        live = jnp.where(stratum_at == s, count[0, s], live)

    def hold_places(first, last):
        for r in range(first, last):
            here = slice(r * LANES, (r + 1) * LANES)
            alive = lane_at + r * LANES < live
            held[:, r, :] = jnp.where(alive, rows[0, :, here], -1).astype(jnp.float32)
            held[:, spans + r, :] = jnp.where(alive, cols[0, :, here], -1).astype(jnp.float32)

    hold_places(0, GROUPS)
    for first in (0, spans):
        tiles[0, first : first + GROUPS] = held[0, first : first + GROUPS]

    parts = ((0, user_count, 0), (user_count, item_count, spans))
    down = lax.broadcasted_iota(jnp.int16, (PACK, LANES), 0)
    across = lax.broadcasted_iota(jnp.int32, (LANES, LANES), 1)
    ones = jnp.ones((PACK, LANES), jnp.bfloat16)
    zeros = jnp.zeros((PACK, LANES), jnp.bfloat16)

    def index_of(s, q, first):
        at = pl.multiple_of(first + q * GROUPS, GROUPS)
        return tiles[s, pl.ds(at, GROUPS), :].astype(jnp.int32)

    def build_chooser(s, q):
        for base, size, first in parts:
            index = index_of(s, q, first)
            for j in range(GROUPS):
                row = jnp.broadcast_to(index[j : j + 1, :], (PACK, LANES)).astype(jnp.int16)
                for t in range(base, base + size, PACK):
                    chooser[t : t + PACK, j * LANES : (j + 1) * LANES] = jnp.where(down == row, ones, zeros)
                    row = row - jnp.int16(PACK)

    def build_spreader(s, q):
        for base, size, first in parts:
            index = jnp.transpose(index_of(s, q, first))
            for j in range(GROUPS):
                column = jnp.broadcast_to(index[:, j : j + 1], (LANES, LANES))
                for t in range(0, size, LANES):
                    spreader[j * LANES : (j + 1) * LANES, base + t : base + t + LANES] = (
                        jnp.where(across + t == column, 1.0, 0.0).astype(jnp.bfloat16)
                    )

    def store_cat(cat, here, block):
        high, low = split_rows(block)
        cat[:depth, here] = high
        cat[depth:, here] = low

    def cut_users(s):
        store_cat(u_cat, slice(None), users[s])

    def tile_copy(s):
        return pltpu.make_async_remote_copy(
            src_ref=held.at[s], dst_ref=tiles.at[s],
            send_sem=tile_send.at[s], recv_sem=tile_recv.at[s],
            device_id=(lax.rem(blk + blocks - s, blocks), rank),
            device_id_type=MESH,
        )

    def user_copy(s):
        return pltpu.make_async_remote_copy(
            src_ref=users.at[s], dst_ref=users.at[s + 1],
            send_sem=user_send.at[s], recv_sem=user_recv.at[s],
            device_id=at_blk(-1), device_id_type=MESH,
        )

    def home():
        return pltpu.make_async_remote_copy(
            src_ref=users.at[strata - 1], dst_ref=u_out,
            send_sem=user_send.at[strata - 1], recv_sem=user_recv.at[strata - 1],
            device_id=at_blk(strata - 1), device_id_type=MESH,
        )

    def part_copy(slot, o):
        return pltpu.make_async_remote_copy(
            src_ref=partial.at[slot], dst_ref=arrived.at[slot, o - 1],
            send_sem=part_send.at[slot, o - 1], recv_sem=part_recv.at[slot, o - 1],
            device_id=at_rank(o), device_id_type=MESH,
        )

    group_at = lax.broadcasted_iota(jnp.int32, (GROUPS, LANES), 0)

    def pick(cat, rows, c):
        both = jnp.dot(cat[...], chooser[rows, c : c + CHUNK], preferred_element_type=jnp.float32)
        return both[:depth] + both[depth:]

    def pick_items():
        for c in range(0, BATCH, CHUNK):
            v_pick[:, c : c + CHUNK] = pick(v_cat, slice(user_count, None), c)

    def pick_users(slot):
        total = jnp.zeros((GROUPS, LANES), jnp.float32)
        for c in range(0, BATCH, CHUNK):
            here = slice(c, c + CHUNK)
            u = pick(u_cat, slice(0, user_count), c)
            u_pick[:, here] = u
            sums = jnp.sum(u * v_pick[:, here], axis=0, keepdims=True)
            for g in range(0, CHUNK, LANES):
                total = jnp.where(group_at == (c + g) // LANES, sums[:, g : g + LANES], total)
        partial[slot] = total

    def send_parts(slot):
        for o in range(1, ranks):
            part_copy(slot, o).start()

    def get_errors(s, q, slot):
        for o in range(1, ranks):
            part_copy(slot, o).wait_recv()
        total = partial[slot]
        for o in range(1, ranks):
            total = total + arrived[slot, o - 1]
        at = pl.multiple_of(2 * spans + q * GROUPS, GROUPS)
        errs[...] = LEARN_RATE * (tiles[s, pl.ds(at, GROUPS), :] - total)

    def make_steps(mine, other, steps):
        for j in range(GROUPS):
            here = slice(j * LANES, (j + 1) * LANES)
            e = errs[j : j + 1, :]
            high, low = split_rows(e * other[:, here] - LEARN_RATE * DECAY_WEIGHT * mine[:, here])
            steps[:depth, here] = high
            steps[depth:, here] = low

    def spread(steps, first):
        moved = jnp.dot(
            steps[...], spreader[:, first : first + CHUNK], preferred_element_type=jnp.float32
        )
        return moved[:depth] + moved[depth:]

    def move_users(s):
        make_steps(u_pick, v_pick, u_step)
        for t in range(0, user_count, CHUNK):
            here = slice(t, t + CHUNK)
            new = users[s, :, here] + spread(u_step, t)
            users[s, :, here] = new
            store_cat(u_cat, here, new)

    def move_items():
        make_steps(v_pick, u_pick, v_step)
        for t in range(0, item_count, CHUNK):
            here = slice(t, t + CHUNK)
            new = v_out[:, here] + spread(v_step, user_count + t)
            v_out[:, here] = new
            store_cat(v_cat, here, new)

    build_chooser(0, 0)
    for load in loads[4:]:
        load.wait()
    cut_users(0)
    store_cat(v_cat, slice(None), v_out[...])
    pick_items()
    pick_users(0)
    pl.semaphore_wait(barrier, len(met))
    send_parts(0)
    hold_places(GROUPS, spans)
    loads[3].wait()
    for r in range(spans):
        held[:, 2 * spans + r, :] = vals[0, :, r * LANES : (r + 1) * LANES]
    tiles[0] = held[0]
    for s in range(1, strata):
        tile_copy(s).start()

    @pl.loop(0, strata)
    def _(s):
        @pl.loop(0, per_tile - 1)
        def _(q):
            slot = (s * per_tile + q) % 2
            build_spreader(s, q)
            build_chooser(s, q + 1)
            get_errors(s, q, slot)
            move_users(s)
            move_items()
            pick_items()
            pick_users(1 - slot)
            send_parts(1 - slot)
            for o in range(1, ranks):
                part_copy(slot, o).wait_send()

        q = per_tile - 1
        slot = (s * per_tile + q) % 2
        build_spreader(s, q)

        @pl.when(s < strata - 1)
        def _():
            tile_copy(s + 1).wait_recv()
            build_chooser(s + 1, 0)

        get_errors(s, q, slot)
        move_users(s)

        @pl.when(s < strata - 1)
        def _():
            user_copy(s).start()

        @pl.when(s == strata - 1)
        def _():
            home().start()

        move_items()
        for o in range(1, ranks):
            part_copy(slot, o).wait_send()

        @pl.when(s < strata - 1)
        def _():
            pick_items()
            user_copy(s).wait()
            cut_users(s + 1)
            pick_users(1 - slot)
            send_parts(1 - slot)

    for s in range(1, strata):
        tile_copy(s).wait_send()
    home().wait()


def solution(mesh):
    blocks, ranks = mesh.shape["blk"], mesh.shape["rank"]

    def per_device(user_factors, item_factors, tile_rows, tile_cols, tile_vals, tile_count):
        depth, user_count = user_factors.shape
        item_count = item_factors.shape[1]
        strata, tile = tile_rows.shape[1:]
        held = (strata, 3 * tile // LANES, LANES)
        vmem = pl.BlockSpec(memory_space=pltpu.VMEM)
        f32, bf16 = jnp.float32, jnp.bfloat16
        return pl.pallas_call(
            functools.partial(kernel, blocks, ranks),
            out_shape=(
                jax.ShapeDtypeStruct((depth, user_count), f32),
                jax.ShapeDtypeStruct((depth, item_count), f32),
            ),
            in_specs=[pl.BlockSpec(memory_space=pl.ANY)] * 6,
            out_specs=(vmem, vmem),
            scratch_shapes=[
                pltpu.VMEM(tile_rows.shape, jnp.int32),
                pltpu.VMEM(tile_cols.shape, jnp.int32),
                pltpu.VMEM(tile_vals.shape, f32),
                pltpu.SMEM(tile_count.shape, jnp.int32),
                pltpu.VMEM((strata, depth, user_count), f32),
                pltpu.VMEM((2 * depth, user_count), bf16),
                pltpu.VMEM((2 * depth, item_count), bf16),
                pltpu.VMEM(held, f32),
                pltpu.VMEM(held, f32),
                pltpu.VMEM((user_count + item_count, BATCH), bf16),
                pltpu.VMEM((BATCH, user_count + item_count), bf16),
                pltpu.VMEM((depth, BATCH), f32),
                pltpu.VMEM((depth, BATCH), f32),
                pltpu.VMEM((2 * depth, BATCH), bf16),
                pltpu.VMEM((2 * depth, BATCH), bf16),
                pltpu.VMEM((2, GROUPS, LANES), f32),
                pltpu.VMEM((2, ranks - 1, GROUPS, LANES), f32),
                pltpu.VMEM((GROUPS, LANES), f32),
                pltpu.SemaphoreType.DMA((2, ranks - 1)),
                pltpu.SemaphoreType.DMA((2, ranks - 1)),
                pltpu.SemaphoreType.DMA((strata,)),
                pltpu.SemaphoreType.DMA((strata,)),
                pltpu.SemaphoreType.DMA((strata,)),
                pltpu.SemaphoreType.DMA((strata,)),
                pltpu.SemaphoreType.DMA((6,)),
            ],
            compiler_params=pltpu.CompilerParams(
                collective_id=0, has_side_effects=True, vmem_limit_bytes=60 * 1024 * 1024
            ),
        )(user_factors, item_factors, tile_rows, tile_cols, tile_vals, tile_count)

    placed = (
        P("rank", "blk"),
        P("rank", "blk"),
        P("blk", None, None),
        P("blk", None, None),
        P("blk", None, None),
        P("blk", None),
    )
    return jax.shard_map(
        per_device,
        mesh=mesh,
        in_specs=placed,
        out_specs=(P("rank", "blk"), P("rank", "blk")),
        check_vma=False,
    )
```

```python
import functools

import jax
import jax.numpy as jnp
from jax import lax
from jax.experimental import pallas as pl
from jax.experimental.pallas import tpu as pltpu
from jax.sharding import PartitionSpec as P

BATCH = 1024
LANES = 128
GROUPS = BATCH // LANES
CHUNK = 256
PACK = 16
LEARN_RATE = 0.05
DECAY_WEIGHT = 0.02
MESH = pl.DeviceIdType.MESH


def split_rows(block):
    high = block.astype(jnp.bfloat16)
    low = (block - high.astype(jnp.float32)).astype(jnp.bfloat16)
    return high, low


def kernel(
    blocks, ranks,
    u_in, v_in, rows_in, cols_in, vals_in, count_in,
    u_out, v_out,
    rows, cols, vals, count, users, u_cat, v_cat, held, tiles, chooser, spreader, u_pick, v_pick, u_step, v_step,
    partial, arrived, errs,
    part_send, part_recv, tile_send, tile_recv, user_send, user_recv, load_sem,
):
    depth, user_count = u_in.shape
    item_count = v_in.shape[1]
    strata, tile = rows_in.shape[1:]
    per_tile = tile // BATCH
    spans = tile // LANES
    blk = lax.axis_index("blk")
    rank = lax.axis_index("rank")

    def at_blk(shift):
        return (lax.rem(blk + (shift % blocks), blocks), rank)

    def at_rank(shift):
        return (blk, lax.rem(rank + (shift % ranks), ranks))

    barrier = pltpu.get_barrier_semaphore()
    met = [at_rank(o) for o in range(1, ranks)]
    met += [at_blk(o) for o in range(1, strata)] + [at_blk(-o) for o in range(1, strata)]
    for device in met:
        pl.semaphore_signal(barrier, inc=1, device_id=device, device_id_type=MESH)

    loads = [
        pltpu.make_async_copy(source, target, load_sem.at[i])
        for i, (source, target) in enumerate(
            (
                (count_in, count), (rows_in, rows), (cols_in, cols), (vals_in, vals),
                (u_in, users.at[0]), (v_in, v_out),
            )
        )
    ]
    for load in loads:
        load.start()
    for load in loads[:3]:
        load.wait()

    stratum_at = lax.broadcasted_iota(jnp.int32, (strata, LANES), 0)
    lane_at = lax.broadcasted_iota(jnp.int32, (strata, LANES), 1)
    live = jnp.zeros((strata, LANES), jnp.int32)
    for s in range(strata):
        live = jnp.where(stratum_at == s, count[0, s], live)

    def hold_places(first, last):
        for r in range(first, last):
            here = slice(r * LANES, (r + 1) * LANES)
            alive = lane_at + r * LANES < live
            held[:, r, :] = jnp.where(alive, rows[0, :, here], -1).astype(jnp.float32)
            held[:, spans + r, :] = jnp.where(alive, cols[0, :, here], -1).astype(jnp.float32)

    hold_places(0, GROUPS)
    for first in (0, spans):
        tiles[0, first : first + GROUPS] = held[0, first : first + GROUPS]

    parts = ((0, user_count, 0), (user_count, item_count, spans))
    down = lax.broadcasted_iota(jnp.int16, (PACK, LANES), 0)
    across = lax.broadcasted_iota(jnp.int32, (LANES, LANES), 1)
    ones = jnp.ones((PACK, LANES), jnp.bfloat16)
    zeros = jnp.zeros((PACK, LANES), jnp.bfloat16)

    def index_of(s, q, first):
        at = pl.multiple_of(first + q * GROUPS, GROUPS)
        return tiles[s, pl.ds(at, GROUPS), :].astype(jnp.int32)

    def build_chooser(s, q):
        for base, size, first in parts:
            index = index_of(s, q, first)
            for j in range(GROUPS):
                row = jnp.broadcast_to(index[j : j + 1, :], (PACK, LANES)).astype(jnp.int16)
                for t in range(base, base + size, PACK):
                    chooser[t : t + PACK, j * LANES : (j + 1) * LANES] = jnp.where(down == row, ones, zeros)
                    row = row - jnp.int16(PACK)

    def build_spreader(s, q):
        for base, size, first in parts:
            index = jnp.transpose(index_of(s, q, first))
            for j in range(GROUPS):
                column = jnp.broadcast_to(index[:, j : j + 1], (LANES, LANES))
                for t in range(0, size, LANES):
                    spreader[j * LANES : (j + 1) * LANES, base + t : base + t + LANES] = (
                        jnp.where(across + t == column, 1.0, 0.0).astype(jnp.bfloat16)
                    )

    def store_cat(cat, here, block):
        high, low = split_rows(block)
        cat[:depth, here] = high
        cat[depth:, here] = low

    def cut_users(s):
        store_cat(u_cat, slice(None), users[s])

    def tile_copy(s):
        return pltpu.make_async_remote_copy(
            src_ref=held.at[s], dst_ref=tiles.at[s],
            send_sem=tile_send.at[s], recv_sem=tile_recv.at[s],
            device_id=(lax.rem(blk + blocks - s, blocks), rank),
            device_id_type=MESH,
        )

    def user_copy(s):
        return pltpu.make_async_remote_copy(
            src_ref=users.at[s], dst_ref=users.at[s + 1],
            send_sem=user_send.at[s], recv_sem=user_recv.at[s],
            device_id=at_blk(-1), device_id_type=MESH,
        )

    def home():
        return pltpu.make_async_remote_copy(
            src_ref=users.at[strata - 1], dst_ref=u_out,
            send_sem=user_send.at[strata - 1], recv_sem=user_recv.at[strata - 1],
            device_id=at_blk(strata - 1), device_id_type=MESH,
        )

    def part_copy(slot, o):
        return pltpu.make_async_remote_copy(
            src_ref=partial.at[slot], dst_ref=arrived.at[slot, o - 1],
            send_sem=part_send.at[slot, o - 1], recv_sem=part_recv.at[slot, o - 1],
            device_id=at_rank(o), device_id_type=MESH,
        )

    group_at = lax.broadcasted_iota(jnp.int32, (GROUPS, LANES), 0)

    def pick(cat, rows, c):
        both = jnp.dot(cat[...], chooser[rows, c : c + CHUNK], preferred_element_type=jnp.float32)
        return both[:depth] + both[depth:]

    def pick_users(c):
        here = slice(c, c + CHUNK)
        u = pick(u_cat, slice(0, user_count), c)
        u_pick[:, here] = u
        return u

    def pick_items(c):
        here = slice(c, c + CHUNK)
        v = pick(v_cat, slice(user_count, None), c)
        v_pick[:, here] = v
        return v

    def predict(slot, users_first):
        first, second = (pick_users, pick_items) if users_first else (pick_items, pick_users)
        other = u_pick if users_first else v_pick
        if users_first:
            for c in range(0, BATCH, CHUNK):
                first(c)
        total = jnp.zeros((GROUPS, LANES), jnp.float32)
        for c in range(0, BATCH, CHUNK):
            sums = jnp.sum(second(c) * other[:, c : c + CHUNK], axis=0, keepdims=True)
            for g in range(0, CHUNK, LANES):
                total = jnp.where(group_at == (c + g) // LANES, sums[:, g : g + LANES], total)
        partial[slot] = total

    def send_parts(slot):
        for o in range(1, ranks):
            part_copy(slot, o).start()

    def get_errors(s, q, slot):
        for o in range(1, ranks):
            part_copy(slot, o).wait_recv()
        total = partial[slot]
        for o in range(1, ranks):
            total = total + arrived[slot, o - 1]
        at = pl.multiple_of(2 * spans + q * GROUPS, GROUPS)
        errs[...] = LEARN_RATE * (tiles[s, pl.ds(at, GROUPS), :] - total)

    def make_steps(mine, other, steps):
        for j in range(GROUPS):
            here = slice(j * LANES, (j + 1) * LANES)
            e = errs[j : j + 1, :]
            high, low = split_rows(e * other[:, here] - LEARN_RATE * DECAY_WEIGHT * mine[:, here])
            steps[:depth, here] = high
            steps[depth:, here] = low

    def spread(steps, first):
        moved = jnp.dot(
            steps[...], spreader[:, first : first + CHUNK], preferred_element_type=jnp.float32
        )
        return moved[:depth] + moved[depth:]

    def move_users(s):
        make_steps(u_pick, v_pick, u_step)
        for t in range(0, user_count, CHUNK):
            here = slice(t, t + CHUNK)
            new = users[s, :, here] + spread(u_step, t)
            users[s, :, here] = new
            store_cat(u_cat, here, new)

    def move_items():
        make_steps(v_pick, u_pick, v_step)
        for t in range(0, item_count, CHUNK):
            here = slice(t, t + CHUNK)
            new = v_out[:, here] + spread(v_step, user_count + t)
            v_out[:, here] = new
            store_cat(v_cat, here, new)

    build_chooser(0, 0)
    for load in loads[4:]:
        load.wait()
    cut_users(0)
    store_cat(v_cat, slice(None), v_out[...])
    predict(0, True)
    pl.semaphore_wait(barrier, len(met))
    send_parts(0)
    hold_places(GROUPS, spans)
    loads[3].wait()
    for r in range(spans):
        held[:, 2 * spans + r, :] = vals[0, :, r * LANES : (r + 1) * LANES]
    tiles[0] = held[0]
    for s in range(1, strata):
        tile_copy(s).start()

    @pl.loop(0, strata)
    def _(s):
        @pl.loop(0, per_tile - 1)
        def _(q):
            slot = (s * per_tile + q) % 2
            build_spreader(s, q)
            build_chooser(s, q + 1)
            get_errors(s, q, slot)
            move_users(s)
            move_items()
            predict(1 - slot, True)
            send_parts(1 - slot)
            for o in range(1, ranks):
                part_copy(slot, o).wait_send()

        q = per_tile - 1
        slot = (s * per_tile + q) % 2
        build_spreader(s, q)

        @pl.when(s < strata - 1)
        def _():
            tile_copy(s + 1).wait_recv()
            build_chooser(s + 1, 0)

        get_errors(s, q, slot)
        move_users(s)

        @pl.when(s < strata - 1)
        def _():
            user_copy(s).start()

        @pl.when(s == strata - 1)
        def _():
            home().start()

        move_items()
        for o in range(1, ranks):
            part_copy(slot, o).wait_send()

        @pl.when(s < strata - 1)
        def _():
            for c in range(0, BATCH, CHUNK):
                pick_items(c)
            user_copy(s).wait()
            cut_users(s + 1)
            predict(1 - slot, False)
            send_parts(1 - slot)

    for s in range(1, strata):
        tile_copy(s).wait_send()
    home().wait()


def hand_over(u_in, v_in, u_out, v_out, sem):
    copies = [
        pltpu.make_async_copy(source, target, sem.at[i])
        for i, (source, target) in enumerate(((v_in, v_out), (u_in, u_out)))
    ]
    for copy in copies:
        copy.start()
    for copy in copies:
        copy.wait()


def solution(mesh):
    blocks, ranks = mesh.shape["blk"], mesh.shape["rank"]

    def per_device(user_factors, item_factors, tile_rows, tile_cols, tile_vals, tile_count):
        depth, user_count = user_factors.shape
        item_count = item_factors.shape[1]
        strata, tile = tile_rows.shape[1:]
        held = (strata, 3 * tile // LANES, LANES)
        vmem = pl.BlockSpec(memory_space=pltpu.VMEM)
        f32, bf16 = jnp.float32, jnp.bfloat16
        moved = pl.pallas_call(
            functools.partial(kernel, blocks, ranks),
            out_shape=(
                pltpu.VMEM((depth, user_count), f32),
                pltpu.VMEM((depth, item_count), f32),
            ),
            in_specs=[pl.BlockSpec(memory_space=pl.ANY)] * 6,
            out_specs=(vmem, vmem),
            scratch_shapes=[
                pltpu.VMEM(tile_rows.shape, jnp.int32),
                pltpu.VMEM(tile_cols.shape, jnp.int32),
                pltpu.VMEM(tile_vals.shape, f32),
                pltpu.SMEM(tile_count.shape, jnp.int32),
                pltpu.VMEM((strata, depth, user_count), f32),
                pltpu.VMEM((2 * depth, user_count), bf16),
                pltpu.VMEM((2 * depth, item_count), bf16),
                pltpu.VMEM(held, f32),
                pltpu.VMEM(held, f32),
                pltpu.VMEM((user_count + item_count, BATCH), bf16),
                pltpu.VMEM((BATCH, user_count + item_count), bf16),
                pltpu.VMEM((depth, BATCH), f32),
                pltpu.VMEM((depth, BATCH), f32),
                pltpu.VMEM((2 * depth, BATCH), bf16),
                pltpu.VMEM((2 * depth, BATCH), bf16),
                pltpu.VMEM((2, GROUPS, LANES), f32),
                pltpu.VMEM((2, ranks - 1, GROUPS, LANES), f32),
                pltpu.VMEM((GROUPS, LANES), f32),
                pltpu.SemaphoreType.DMA((2, ranks - 1)),
                pltpu.SemaphoreType.DMA((2, ranks - 1)),
                pltpu.SemaphoreType.DMA((strata,)),
                pltpu.SemaphoreType.DMA((strata,)),
                pltpu.SemaphoreType.DMA((strata,)),
                pltpu.SemaphoreType.DMA((strata,)),
                pltpu.SemaphoreType.DMA((6,)),
            ],
            compiler_params=pltpu.CompilerParams(
                collective_id=0, has_side_effects=True, vmem_limit_bytes=60 * 1024 * 1024
            ),
        )(user_factors, item_factors, tile_rows, tile_cols, tile_vals, tile_count)
        return pl.pallas_call(
            hand_over,
            out_shape=(
                jax.ShapeDtypeStruct((depth, user_count), f32),
                jax.ShapeDtypeStruct((depth, item_count), f32),
            ),
            in_specs=[vmem, vmem],
            out_specs=[pl.BlockSpec(memory_space=pl.ANY)] * 2,
            scratch_shapes=[pltpu.SemaphoreType.DMA((2,))],
        )(*[pltpu.with_memory_space_constraint(x, pltpu.VMEM) for x in moved])

    placed = (
        P("rank", "blk"),
        P("rank", "blk"),
        P("blk", None, None),
        P("blk", None, None),
        P("blk", None, None),
        P("blk", None),
    )
    return jax.shard_map(
        per_device,
        mesh=mesh,
        in_specs=placed,
        out_specs=(P("rank", "blk"), P("rank", "blk")),
        check_vma=False,
    )
```

```python
import functools

import jax
import jax.numpy as jnp
from jax import lax
from jax.experimental import pallas as pl
from jax.experimental.pallas import tpu as pltpu
from jax.sharding import PartitionSpec as P

BATCH = 1024
LANES = 128
GROUPS = BATCH // LANES
CHUNK = 256
PACK = 16
FOLD = 2
LEARN_RATE = 0.05
DECAY_WEIGHT = 0.02
MESH = pl.DeviceIdType.MESH


def split_rows(block):
    high = block.astype(jnp.bfloat16)
    low = (block - high.astype(jnp.float32)).astype(jnp.bfloat16)
    return high, low


def kernel(
    blocks, ranks,
    u_in, v_in, rows_in, cols_in, vals_in, count_in,
    u_out, v_out,
    rows, cols, vals, count, users, u_cat, v_cat, held, tiles, chooser, sides, spreader, u_pick, v_pick, u_next, v_next,
    u_step, v_step, u_turn, v_turn,
    partial, arrived, errs,
    part_send, part_recv, tile_send, tile_recv, user_send, user_recv, load_sem,
):
    depth, user_count = u_in.shape
    item_count = v_in.shape[1]
    strata, tile = rows_in.shape[1:]
    per_tile = tile // BATCH
    spans = tile // LANES
    user_keys = user_count // FOLD
    item_keys = item_count // FOLD
    blk = lax.axis_index("blk")
    rank = lax.axis_index("rank")

    def at_blk(shift):
        return (lax.rem(blk + (shift % blocks), blocks), rank)

    def at_rank(shift):
        return (blk, lax.rem(rank + (shift % ranks), ranks))

    loads = [
        pltpu.make_async_copy(source, target, load_sem.at[i])
        for i, (source, target) in enumerate(
            (
                (count_in, count), (rows_in, rows), (cols_in, cols), (vals_in, vals),
                (u_in, users.at[0]), (v_in, v_out),
            )
        )
    ]
    for load in loads:
        load.start()
    barrier = pltpu.get_barrier_semaphore()
    met = [at_rank(o) for o in range(1, ranks)]
    met += [at_blk(o) for o in range(1, strata)] + [at_blk(-o) for o in range(1, strata)]
    for device in met:
        pl.semaphore_signal(barrier, inc=1, device_id=device, device_id_type=MESH)
    for i in (0, 1, 2, 4, 5):
        loads[i].wait()

    stratum_at = lax.broadcasted_iota(jnp.int32, (strata, LANES), 0)
    lane_at = lax.broadcasted_iota(jnp.int32, (strata, LANES), 1)
    live = jnp.zeros((strata, LANES), jnp.int32)
    for s in range(strata):
        live = jnp.where(stratum_at == s, count[0, s], live)

    def hold_places(first, last):
        for r in range(first, last):
            here = slice(r * LANES, (r + 1) * LANES)
            alive = lane_at + r * LANES < live
            held[:, r, :] = jnp.where(alive, rows[0, :, here], -1).astype(jnp.float32)
            held[:, spans + r, :] = jnp.where(alive, cols[0, :, here], -1).astype(jnp.float32)

    hold_places(0, GROUPS)
    for first in (0, spans):
        tiles[0, first : first + GROUPS] = held[0, first : first + GROUPS]

    parts = ((0, user_count, 0), (user_count, item_count, spans))
    down = lax.broadcasted_iota(jnp.int16, (PACK, LANES), 0)
    across = lax.broadcasted_iota(jnp.int32, (LANES, LANES), 1)
    ones = jnp.ones((PACK, LANES), jnp.bfloat16)
    zeros = jnp.zeros((PACK, LANES), jnp.bfloat16)

    def index_of(s, q, first):
        at = pl.multiple_of(first + q * GROUPS, GROUPS)
        return tiles[s, pl.ds(at, GROUPS), :].astype(jnp.int32)

    folded = ((0, user_keys, 0, 0), (1, item_keys, spans, user_keys))

    def build_chooser(s, q, wanted=folded):
        for p, size, first, base in wanted:
            index = index_of(s, q, first)
            side = index >= size
            sides[p] = jnp.where(side, 1.0, 0.0)
            index = jnp.where(side, index - size, index)
            for j in range(GROUPS):
                row = jnp.broadcast_to(index[j : j + 1, :], (PACK, LANES)).astype(jnp.int16)
                for t in range(base, base + size, PACK):
                    chooser[t : t + PACK, j * LANES : (j + 1) * LANES] = jnp.where(down == row, ones, zeros)
                    row = row - jnp.int16(PACK)

    def build_spreader(s, q):
        for base, size, first in parts:
            index = jnp.transpose(index_of(s, q, first))
            for j in range(GROUPS):
                column = jnp.broadcast_to(index[:, j : j + 1], (LANES, LANES))
                for t in range(0, size, LANES):
                    spreader[j * LANES : (j + 1) * LANES, base + t : base + t + LANES] = (
                        jnp.where(across + t == column, 1.0, 0.0).astype(jnp.bfloat16)
                    )

    def fold(cat, t, pieces):
        keys = cat.shape[1]
        b, at = t // keys, t % keys
        for i, piece in enumerate(pieces):
            row = (b * len(pieces) + i) * depth
            cat[row : row + depth, at : at + CHUNK] = piece

    def cut_users(s, t):
        fold(u_cat, t, split_rows(users[s, :, t : t + CHUNK]))

    def cut_items():
        for t in range(0, item_count, CHUNK):
            fold(v_cat, t, split_rows(v_out[:, t : t + CHUNK]))

    def tile_copy(s):
        return pltpu.make_async_remote_copy(
            src_ref=held.at[s], dst_ref=tiles.at[s],
            send_sem=tile_send.at[s], recv_sem=tile_recv.at[s],
            device_id=(lax.rem(blk + blocks - s, blocks), rank),
            device_id_type=MESH,
        )

    def user_copy(s, t):
        here = slice(t, t + CHUNK)
        return pltpu.make_async_remote_copy(
            src_ref=users.at[s, :, here], dst_ref=users.at[s + 1, :, here],
            send_sem=user_send.at[s, t // CHUNK], recv_sem=user_recv.at[s, t // CHUNK],
            device_id=at_blk(-1), device_id_type=MESH,
        )

    def home(t):
        here = slice(t, t + CHUNK)
        return pltpu.make_async_remote_copy(
            src_ref=users.at[strata - 1, :, here], dst_ref=u_out.at[:, here],
            send_sem=user_send.at[strata - 1, t // CHUNK], recv_sem=user_recv.at[strata - 1, t // CHUNK],
            device_id=at_blk(strata - 1), device_id_type=MESH,
        )

    def part_copy(slot, o):
        return pltpu.make_async_remote_copy(
            src_ref=partial.at[slot], dst_ref=arrived.at[slot, o - 1],
            send_sem=part_send.at[slot, o - 1], recv_sem=part_recv.at[slot, o - 1],
            device_id=at_rank(o), device_id_type=MESH,
        )

    group_at = lax.broadcasted_iota(jnp.int32, (GROUPS, LANES), 0)

    user_rows, item_rows = slice(0, user_keys), slice(user_keys, user_keys + item_keys)

    def pick(cat, p, c):
        rows = (user_rows, item_rows)[p]
        both = jnp.dot(cat[...], chooser[rows, c : c + CHUNK], preferred_element_type=jnp.float32)
        found = []
        for g in range(0, CHUNK, LANES):
            j = (c + g) // LANES
            at = both[:, g : g + LANES]
            half = at.shape[0] // 2
            first, second = at[:half], at[half:]
            if half > depth:
                first, second = first[:depth] + first[depth:], second[:depth] + second[depth:]
            side = jnp.broadcast_to(sides[p, j : j + 1, :], (depth, LANES)) > 0.5
            found.append(jnp.where(side, second, first))
        return found

    def pick_whole(cat, p, target, c):
        for g, found in enumerate(pick(cat, p, c)):
            target[:, c + g * LANES : c + (g + 1) * LANES] = found

    def pick_moved(turned, p, stale, target, c):
        for g, found in enumerate(pick(turned, p, c)):
            here = slice(c + g * LANES, c + (g + 1) * LANES)
            target[:, here] = stale[:, here] + found

    def sum_parts(slot, pick_last):
        total = jnp.zeros((GROUPS, LANES), jnp.float32)
        for c in range(0, BATCH, CHUNK):
            pick_last(c)
            for j in range(c // LANES, (c + CHUNK) // LANES):
                here = slice(j * LANES, (j + 1) * LANES)
                sums = jnp.sum(u_pick[:, here] * v_pick[:, here], axis=0, keepdims=True)
                total = jnp.where(group_at == j, sums, total)
        partial[slot] = total

    chunks = range(0, BATCH, CHUNK)

    def send_parts(slot):
        for o in sorted(range(1, ranks), key=lambda o: abs(o - ranks // 2)):
            part_copy(slot, o).start()

    def get_errors(s, q, slot):
        for o in range(1, ranks):
            part_copy(slot, o).wait_recv()
        total = partial[slot]
        for o in range(1, ranks):
            total = total + arrived[slot, o - 1]
        at = pl.multiple_of(2 * spans + q * GROUPS, GROUPS)
        errs[...] = LEARN_RATE * (tiles[s, pl.ds(at, GROUPS), :] - total)

    def make_steps(mine, other, steps):
        for j in range(GROUPS):
            here = slice(j * LANES, (j + 1) * LANES)
            e = errs[j : j + 1, :]
            high, low = split_rows(e * other[:, here] - LEARN_RATE * DECAY_WEIGHT * mine[:, here])
            steps[:depth, here] = high
            steps[depth:, here] = low

    def spread(steps, first):
        moved = jnp.dot(
            steps[...], spreader[:, first : first + CHUNK], preferred_element_type=jnp.float32
        )
        return moved[:depth] + moved[depth:]

    def move_users(s, t):
        here = slice(t, t + CHUNK)
        moved = spread(u_step, t)
        users[s, :, here] += moved
        return moved

    def move_items(t):
        here = slice(t, t + CHUNK)
        moved = spread(v_step, user_count + t)
        v_out[:, here] += moved
        return moved

    for t in range(0, user_count, CHUNK):
        cut_users(0, t)
    build_chooser(0, 0, folded[:1])
    for c in chunks:
        pick_whole(u_cat, 0, u_pick, c)
    cut_items()
    build_chooser(0, 0, folded[1:])
    sum_parts(0, lambda c: pick_whole(v_cat, 1, v_pick, c))
    pl.semaphore_wait(barrier, len(met))
    send_parts(0)
    hold_places(GROUPS, spans)
    loads[3].wait()
    for r in range(spans):
        held[:, 2 * spans + r, :] = vals[0, :, r * LANES : (r + 1) * LANES]
    tiles[0] = held[0]
    for s in range(1, strata):
        tile_copy(s).start()

    @pl.loop(0, strata)
    def _(s):
        @pl.loop(0, per_tile - 1)
        def _(q):
            slot = (s * per_tile + q) % 2
            for t in range(0, user_count, CHUNK):
                cut_users(s, t)
            cut_items()
            build_chooser(s, q + 1)
            for c in chunks:
                pick_whole(u_cat, 0, u_next, c)
                pick_whole(v_cat, 1, v_next, c)
            build_spreader(s, q)
            get_errors(s, q, slot)
            make_steps(u_pick, v_pick, u_step)
            for t in range(0, user_count, CHUNK):
                fold(u_turn, t, [move_users(s, t).astype(jnp.bfloat16)])
            make_steps(v_pick, u_pick, v_step)
            for t in range(0, item_count, CHUNK):
                fold(v_turn, t, [move_items(t).astype(jnp.bfloat16)])
            for c in chunks:
                pick_moved(u_turn, 0, u_next, u_pick, c)
            sum_parts(1 - slot, lambda c: pick_moved(v_turn, 1, v_next, v_pick, c))
            send_parts(1 - slot)
            for o in range(1, ranks):
                part_copy(slot, o).wait_send()

        q = per_tile - 1
        slot = (s * per_tile + q) % 2
        build_spreader(s, q)

        @pl.when(s < strata - 1)
        def _():
            tile_copy(s + 1).wait_recv()
            build_chooser(s + 1, 0)

        get_errors(s, q, slot)
        make_steps(u_pick, v_pick, u_step)
        for t in range(0, user_count, CHUNK):
            move_users(s, t)

            @pl.when(s < strata - 1)
            def _():
                user_copy(s, t).start()

            @pl.when(s == strata - 1)
            def _():
                home(t).start()

        make_steps(v_pick, u_pick, v_step)
        for t in range(0, item_count, CHUNK):
            move_items(t)
        for o in range(1, ranks):
            part_copy(slot, o).wait_send()

        @pl.when(s < strata - 1)
        def _():
            cut_items()
            for c in chunks:
                pick_whole(v_cat, 1, v_pick, c)
            for t in range(0, user_count, CHUNK):
                user_copy(s, t).wait()
                cut_users(s + 1, t)
            sum_parts(1 - slot, lambda c: pick_whole(u_cat, 0, u_pick, c))
            send_parts(1 - slot)

    for s in range(1, strata):
        tile_copy(s).wait_send()
    for t in range(0, user_count, CHUNK):
        home(t).wait()


def hand_over(u_in, v_in, u_out, v_out, sem):
    copies = [
        pltpu.make_async_copy(source, target, sem.at[i])
        for i, (source, target) in enumerate(((v_in, v_out), (u_in, u_out)))
    ]
    for copy in copies:
        copy.start()
    for copy in copies:
        copy.wait()


def solution(mesh):
    blocks, ranks = mesh.shape["blk"], mesh.shape["rank"]

    def per_device(user_factors, item_factors, tile_rows, tile_cols, tile_vals, tile_count):
        depth, user_count = user_factors.shape
        item_count = item_factors.shape[1]
        strata, tile = tile_rows.shape[1:]
        held = (strata, 3 * tile // LANES, LANES)
        vmem = pl.BlockSpec(memory_space=pltpu.VMEM)
        f32, bf16 = jnp.float32, jnp.bfloat16
        moved = pl.pallas_call(
            functools.partial(kernel, blocks, ranks),
            out_shape=(
                pltpu.VMEM((depth, user_count), f32),
                pltpu.VMEM((depth, item_count), f32),
            ),
            in_specs=[pl.BlockSpec(memory_space=pl.ANY)] * 6,
            out_specs=(vmem, vmem),
            scratch_shapes=[
                pltpu.VMEM(tile_rows.shape, jnp.int32),
                pltpu.VMEM(tile_cols.shape, jnp.int32),
                pltpu.VMEM(tile_vals.shape, f32),
                pltpu.SMEM(tile_count.shape, jnp.int32),
                pltpu.VMEM((strata, depth, user_count), f32),
                pltpu.VMEM((2 * FOLD * depth, user_count // FOLD), bf16),
                pltpu.VMEM((2 * FOLD * depth, item_count // FOLD), bf16),
                pltpu.VMEM(held, f32),
                pltpu.VMEM(held, f32),
                pltpu.VMEM(((user_count + item_count) // FOLD, BATCH), bf16),
                pltpu.VMEM((2, GROUPS, LANES), f32),
                pltpu.VMEM((BATCH, user_count + item_count), bf16),
                pltpu.VMEM((depth, BATCH), f32),
                pltpu.VMEM((depth, BATCH), f32),
                pltpu.VMEM((depth, BATCH), f32),
                pltpu.VMEM((depth, BATCH), f32),
                pltpu.VMEM((2 * depth, BATCH), bf16),
                pltpu.VMEM((2 * depth, BATCH), bf16),
                pltpu.VMEM((FOLD * depth, user_count // FOLD), bf16),
                pltpu.VMEM((FOLD * depth, item_count // FOLD), bf16),
                pltpu.VMEM((2, GROUPS, LANES), f32),
                pltpu.VMEM((2, ranks - 1, GROUPS, LANES), f32),
                pltpu.VMEM((GROUPS, LANES), f32),
                pltpu.SemaphoreType.DMA((2, ranks - 1)),
                pltpu.SemaphoreType.DMA((2, ranks - 1)),
                pltpu.SemaphoreType.DMA((strata,)),
                pltpu.SemaphoreType.DMA((strata,)),
                pltpu.SemaphoreType.DMA((strata, user_count // CHUNK)),
                pltpu.SemaphoreType.DMA((strata, user_count // CHUNK)),
                pltpu.SemaphoreType.DMA((6,)),
            ],
            compiler_params=pltpu.CompilerParams(
                collective_id=0, has_side_effects=True, vmem_limit_bytes=60 * 1024 * 1024
            ),
        )(user_factors, item_factors, tile_rows, tile_cols, tile_vals, tile_count)
        return pl.pallas_call(
            hand_over,
            out_shape=(
                jax.ShapeDtypeStruct((depth, user_count), f32),
                jax.ShapeDtypeStruct((depth, item_count), f32),
            ),
            in_specs=[vmem, vmem],
            out_specs=[pl.BlockSpec(memory_space=pl.ANY)] * 2,
            scratch_shapes=[pltpu.SemaphoreType.DMA((2,))],
        )(*[pltpu.with_memory_space_constraint(x, pltpu.VMEM) for x in moved])

    placed = (
        P("rank", "blk"),
        P("rank", "blk"),
        P("blk", None, None),
        P("blk", None, None),
        P("blk", None, None),
        P("blk", None),
    )
    return jax.shard_map(
        per_device,
        mesh=mesh,
        in_specs=placed,
        out_specs=(P("rank", "blk"), P("rank", "blk")),
        check_vma=False,
    )
```

```python
import functools

import jax
import jax.numpy as jnp
from jax import lax
from jax.experimental import pallas as pl
from jax.experimental.pallas import tpu as pltpu
from jax.sharding import PartitionSpec as P

BATCH = 1024
LANES = 128
GROUPS = BATCH // LANES
CHUNK = 256
PACK = 16
FOLD = 2
LEARN_RATE = 0.05
DECAY_WEIGHT = 0.02
MESH = pl.DeviceIdType.MESH


def split_rows(block):
    high = block.astype(jnp.bfloat16)
    low = (block - high.astype(jnp.float32)).astype(jnp.bfloat16)
    return high, low


def kernel(
    blocks, ranks,
    u_in, v_in, rows_in, cols_in, vals_in, count_in,
    u_out, v_out,
    rows, cols, vals, count, users, u_cat, v_cat, held, tiles, chooser, sides, spreader, u_pick, v_pick,
    u_step, v_step, u_turn, v_turn, u_moved, v_moved,
    partial, arrived, errs,
    part_send, part_recv, tile_send, tile_recv, user_send, user_recv, load_sem,
):
    depth, user_count = u_in.shape
    item_count = v_in.shape[1]
    strata, tile = rows_in.shape[1:]
    per_tile = tile // BATCH
    spans = tile // LANES
    user_keys = user_count // FOLD
    item_keys = item_count // FOLD
    blk = lax.axis_index("blk")
    rank = lax.axis_index("rank")

    def at_blk(shift):
        return (lax.rem(blk + (shift % blocks), blocks), rank)

    def at_rank(shift):
        return (blk, lax.rem(rank + (shift % ranks), ranks))

    loads = [
        pltpu.make_async_copy(source, target, load_sem.at[i])
        for i, (source, target) in enumerate(
            (
                (count_in, count), (rows_in, rows), (cols_in, cols), (vals_in, vals),
                (u_in, users.at[0]), (v_in, v_out),
            )
        )
    ]
    for load in loads:
        load.start()
    barrier = pltpu.get_barrier_semaphore()
    met = [at_rank(o) for o in range(1, ranks)]
    met += [at_blk(o) for o in range(1, strata)] + [at_blk(-o) for o in range(1, strata)]
    for device in met:
        pl.semaphore_signal(barrier, inc=1, device_id=device, device_id_type=MESH)
    for i in (0, 1, 2, 4, 5):
        loads[i].wait()

    stratum_at = lax.broadcasted_iota(jnp.int32, (strata, LANES), 0)
    lane_at = lax.broadcasted_iota(jnp.int32, (strata, LANES), 1)
    live = jnp.zeros((strata, LANES), jnp.int32)
    for s in range(strata):
        live = jnp.where(stratum_at == s, count[0, s], live)

    def hold_places(first, last):
        for r in range(first, last):
            here = slice(r * LANES, (r + 1) * LANES)
            alive = lane_at + r * LANES < live
            held[:, r, :] = jnp.where(alive, rows[0, :, here], -1).astype(jnp.float32)
            held[:, spans + r, :] = jnp.where(alive, cols[0, :, here], -1).astype(jnp.float32)

    hold_places(0, GROUPS)
    for first in (0, spans):
        tiles[0, first : first + GROUPS] = held[0, first : first + GROUPS]

    parts = ((0, user_count, 0), (user_count, item_count, spans))
    down = lax.broadcasted_iota(jnp.int16, (PACK, LANES), 0)
    across = lax.broadcasted_iota(jnp.int32, (LANES, LANES), 1)
    ones = jnp.ones((PACK, LANES), jnp.bfloat16)
    zeros = jnp.zeros((PACK, LANES), jnp.bfloat16)

    def index_of(s, q, first):
        at = pl.multiple_of(first + q * GROUPS, GROUPS)
        return tiles[s, pl.ds(at, GROUPS), :].astype(jnp.int32)

    folded = ((0, user_keys, 0, 0), (1, item_keys, spans, user_keys))

    def build_chooser(slot, s, q, wanted=folded):
        for p, size, first, base in wanted:
            index = index_of(s, q, first)
            side = index >= size
            sides[slot, p] = jnp.where(side, 1.0, 0.0)
            index = jnp.where(side, index - size, index)
            for j in range(GROUPS):
                row = jnp.broadcast_to(index[j : j + 1, :], (PACK, LANES)).astype(jnp.int16)
                for t in range(base, base + size, PACK):
                    chooser[t : t + PACK, j * LANES : (j + 1) * LANES] = jnp.where(down == row, ones, zeros)
                    row = row - jnp.int16(PACK)

    def build_spreader(s, q):
        for p, size, first, base in folded:
            index = index_of(s, q, first)
            index = jnp.transpose(jnp.where(index >= size, index - size, index))
            for j in range(GROUPS):
                column = jnp.broadcast_to(index[:, j : j + 1], (LANES, LANES))
                for t in range(0, size, LANES):
                    spreader[j * LANES : (j + 1) * LANES, base + t : base + t + LANES] = (
                        jnp.where(across + t == column, 1.0, 0.0).astype(jnp.bfloat16)
                    )

    def fold(cat, t, pieces):
        keys = cat.shape[1]
        b, at = t // keys, t % keys
        for i, piece in enumerate(pieces):
            row = (b * len(pieces) + i) * depth
            cat[row : row + depth, at : at + CHUNK] = piece

    def cut_users(s, t):
        fold(u_cat, t, split_rows(users[s, :, t : t + CHUNK]))

    def cut_items():
        for t in range(0, item_count, CHUNK):
            fold(v_cat, t, split_rows(v_out[:, t : t + CHUNK]))

    def tile_copy(s):
        return pltpu.make_async_remote_copy(
            src_ref=held.at[s], dst_ref=tiles.at[s],
            send_sem=tile_send.at[s], recv_sem=tile_recv.at[s],
            device_id=(lax.rem(blk + blocks - s, blocks), rank),
            device_id_type=MESH,
        )

    def user_copy(s, t):
        here = slice(t, t + CHUNK)
        return pltpu.make_async_remote_copy(
            src_ref=users.at[s, :, here], dst_ref=users.at[s + 1, :, here],
            send_sem=user_send.at[s, t // CHUNK], recv_sem=user_recv.at[s, t // CHUNK],
            device_id=at_blk(-1), device_id_type=MESH,
        )

    def home(t):
        here = slice(t, t + CHUNK)
        return pltpu.make_async_remote_copy(
            src_ref=users.at[strata - 1, :, here], dst_ref=u_out.at[:, here],
            send_sem=user_send.at[strata - 1, t // CHUNK], recv_sem=user_recv.at[strata - 1, t // CHUNK],
            device_id=at_blk(strata - 1), device_id_type=MESH,
        )

    def part_copy(slot, o):
        return pltpu.make_async_remote_copy(
            src_ref=partial.at[slot], dst_ref=arrived.at[slot, o - 1],
            send_sem=part_send.at[slot, o - 1], recv_sem=part_recv.at[slot, o - 1],
            device_id=at_rank(o), device_id_type=MESH,
        )

    group_at = lax.broadcasted_iota(jnp.int32, (GROUPS, LANES), 0)

    user_rows, item_rows = slice(0, user_keys), slice(user_keys, user_keys + item_keys)

    def side_of(slot, p, j):
        return jnp.broadcast_to(sides[slot, p, j : j + 1, :], (depth, LANES))

    def pick(cat, slot, p, c):
        rows = (user_rows, item_rows)[p]
        both = jnp.dot(cat[...], chooser[rows, c : c + CHUNK], preferred_element_type=jnp.float32)
        found = []
        for g in range(0, CHUNK, LANES):
            at = both[:, g : g + LANES]
            half = at.shape[0] // 2
            first, second = at[:half], at[half:]
            if half > depth:
                first, second = first[:depth] + first[depth:], second[:depth] + second[depth:]
            found.append(jnp.where(side_of(slot, p, (c + g) // LANES) > 0.5, second, first))
        return found

    def pick_whole(cat, slot, p, target, c):
        for g, found in enumerate(pick(cat, slot, p, c)):
            target[slot, :, c + g * LANES : c + (g + 1) * LANES] = found

    def pick_moved(turned, slot, p, target, c):
        for g, found in enumerate(pick(turned, slot, p, c)):
            here = slice(c + g * LANES, c + (g + 1) * LANES)
            target[slot, :, here] += found

    def sum_parts(slot, pick_last):
        total = jnp.zeros((GROUPS, LANES), jnp.float32)
        for c in range(0, BATCH, CHUNK):
            pick_last(c)
            for j in range(c // LANES, (c + CHUNK) // LANES):
                here = slice(j * LANES, (j + 1) * LANES)
                sums = jnp.sum(u_pick[slot, :, here] * v_pick[slot, :, here], axis=0, keepdims=True)
                total = jnp.where(group_at == j, sums, total)
        partial[slot] = total

    chunks = range(0, BATCH, CHUNK)

    def send_parts(slot):
        for o in sorted(range(1, ranks), key=lambda o: abs(o - ranks // 2)):
            part_copy(slot, o).start()

    def get_errors(s, q, slot):
        for o in range(1, ranks):
            part_copy(slot, o).wait_recv()
        total = partial[slot]
        for o in range(1, ranks):
            total = total + arrived[slot, o - 1]
        at = pl.multiple_of(2 * spans + q * GROUPS, GROUPS)
        errs[...] = LEARN_RATE * (tiles[s, pl.ds(at, GROUPS), :] - total)

    def make_steps(slot, p, steps, wanted=(0, 1)):
        mine, other = ((u_pick, v_pick), (v_pick, u_pick))[p]
        for j in range(GROUPS):
            here = slice(j * LANES, (j + 1) * LANES)
            e = errs[j : j + 1, :]
            pieces = split_rows(e * other[slot, :, here] - LEARN_RATE * DECAY_WEIGHT * mine[slot, :, here])
            side = side_of(slot, p, j).astype(jnp.bfloat16)
            for w in wanted:
                second = pieces[w] * side
                row = FOLD * depth * w
                steps[row : row + depth, here] = pieces[w] - second
                steps[row + depth : row + 2 * depth, here] = second

    def spread(steps, first):
        return jnp.dot(steps, spreader[:, first : first + CHUNK], preferred_element_type=jnp.float32)

    def add_users(s, t, change):
        for b in range(FOLD):
            here = slice(b * user_keys + t, b * user_keys + t + CHUNK)
            users[s, :, here] += change[b * depth : (b + 1) * depth]

    def add_items(t, change):
        for b in range(FOLD):
            here = slice(b * item_keys + t, b * item_keys + t + CHUNK)
            v_out[:, here] += change[b * depth : (b + 1) * depth]

    highs, lows = slice(0, FOLD * depth), slice(FOLD * depth, 2 * FOLD * depth)

    def spread_both(steps, first):
        change = spread(steps[...], first)
        return change[highs] + change[lows]

    def turn_part(steps, base, t, moved, turned):
        change = spread(steps[highs], base + t)
        moved[:, t : t + CHUNK] = change
        turned[:, t : t + CHUNK] = change.astype(jnp.bfloat16)

    for t in range(0, user_count, CHUNK):
        cut_users(0, t)
    build_chooser(0, 0, 0, folded[:1])
    for c in chunks:
        pick_whole(u_cat, 0, 0, u_pick, c)
    cut_items()
    build_chooser(0, 0, 0, folded[1:])
    sum_parts(0, lambda c: pick_whole(v_cat, 0, 1, v_pick, c))
    pl.semaphore_wait(barrier, len(met))
    send_parts(0)
    hold_places(GROUPS, spans)
    loads[3].wait()
    for r in range(spans):
        held[:, 2 * spans + r, :] = vals[0, :, r * LANES : (r + 1) * LANES]
    tiles[0] = held[0]
    for s in range(1, strata):
        tile_copy(s).start()

    @pl.loop(0, strata)
    def _(s):
        @pl.loop(0, per_tile - 1)
        def _(q):
            slot = (s * per_tile + q) % 2
            build_chooser(1 - slot, s, q + 1)
            for c in chunks:
                pick_whole(u_cat, 1 - slot, 0, u_pick, c)
                pick_whole(v_cat, 1 - slot, 1, v_pick, c)
            build_spreader(s, q)
            get_errors(s, q, slot)
            make_steps(slot, 0, u_step, (0,))
            for t in range(0, user_keys, CHUNK):
                turn_part(u_step, 0, t, u_moved, u_turn)
            make_steps(slot, 1, v_step, (0,))
            for t in range(0, item_keys, CHUNK):
                turn_part(v_step, user_keys, t, v_moved, v_turn)
            for c in chunks:
                pick_moved(u_turn, 1 - slot, 0, u_pick, c)
            sum_parts(1 - slot, lambda c: pick_moved(v_turn, 1 - slot, 1, v_pick, c))
            send_parts(1 - slot)
            make_steps(slot, 0, u_step, (1,))
            make_steps(slot, 1, v_step, (1,))
            for t in range(0, user_keys, CHUNK):
                add_users(s, t, u_moved[:, t : t + CHUNK] + spread(u_step[lows], t))
            for t in range(0, user_count, CHUNK):
                cut_users(s, t)
            for t in range(0, item_keys, CHUNK):
                add_items(t, v_moved[:, t : t + CHUNK] + spread(v_step[lows], user_keys + t))
            cut_items()
            for o in range(1, ranks):
                part_copy(slot, o).wait_send()

        q = per_tile - 1
        slot = (s * per_tile + q) % 2
        build_spreader(s, q)

        @pl.when(s < strata - 1)
        def _():
            tile_copy(s + 1).wait_recv()
            build_chooser(1 - slot, s + 1, 0)

        get_errors(s, q, slot)
        make_steps(slot, 0, u_step)
        for t in range(0, user_keys, CHUNK):
            add_users(s, t, spread_both(u_step, t))

        @pl.when(s < strata - 1)
        def _():
            for t in range(0, user_count, CHUNK):
                user_copy(s, t).start()

        @pl.when(s == strata - 1)
        def _():
            for t in range(0, user_count, CHUNK):
                home(t).start()

        make_steps(slot, 1, v_step)
        for t in range(0, item_keys, CHUNK):
            add_items(t, spread_both(v_step, user_keys + t))
        for o in range(1, ranks):
            part_copy(slot, o).wait_send()

        @pl.when(s < strata - 1)
        def _():
            cut_items()
            for c in chunks:
                pick_whole(v_cat, 1 - slot, 1, v_pick, c)
            for t in range(0, user_count, CHUNK):
                user_copy(s, t).wait()
                cut_users(s + 1, t)
            sum_parts(1 - slot, lambda c: pick_whole(u_cat, 1 - slot, 0, u_pick, c))
            send_parts(1 - slot)

    for s in range(1, strata):
        tile_copy(s).wait_send()
    for t in range(0, user_count, CHUNK):
        home(t).wait()


def hand_over(u_in, v_in, u_out, v_out, sem):
    copies = [
        pltpu.make_async_copy(source, target, sem.at[i])
        for i, (source, target) in enumerate(((v_in, v_out), (u_in, u_out)))
    ]
    for copy in copies:
        copy.start()
    for copy in copies:
        copy.wait()


def solution(mesh):
    blocks, ranks = mesh.shape["blk"], mesh.shape["rank"]

    def per_device(user_factors, item_factors, tile_rows, tile_cols, tile_vals, tile_count):
        depth, user_count = user_factors.shape
        item_count = item_factors.shape[1]
        strata, tile = tile_rows.shape[1:]
        held = (strata, 3 * tile // LANES, LANES)
        vmem = pl.BlockSpec(memory_space=pltpu.VMEM)
        f32, bf16 = jnp.float32, jnp.bfloat16
        moved = pl.pallas_call(
            functools.partial(kernel, blocks, ranks),
            out_shape=(
                pltpu.VMEM((depth, user_count), f32),
                pltpu.VMEM((depth, item_count), f32),
            ),
            in_specs=[pl.BlockSpec(memory_space=pl.ANY)] * 6,
            out_specs=(vmem, vmem),
            scratch_shapes=[
                pltpu.VMEM(tile_rows.shape, jnp.int32),
                pltpu.VMEM(tile_cols.shape, jnp.int32),
                pltpu.VMEM(tile_vals.shape, f32),
                pltpu.SMEM(tile_count.shape, jnp.int32),
                pltpu.VMEM((strata, depth, user_count), f32),
                pltpu.VMEM((2 * FOLD * depth, user_count // FOLD), bf16),
                pltpu.VMEM((2 * FOLD * depth, item_count // FOLD), bf16),
                pltpu.VMEM(held, f32),
                pltpu.VMEM(held, f32),
                pltpu.VMEM(((user_count + item_count) // FOLD, BATCH), bf16),
                pltpu.VMEM((2, 2, GROUPS, LANES), f32),
                pltpu.VMEM((BATCH, (user_count + item_count) // FOLD), bf16),
                pltpu.VMEM((2, depth, BATCH), f32),
                pltpu.VMEM((2, depth, BATCH), f32),
                pltpu.VMEM((2 * FOLD * depth, BATCH), bf16),
                pltpu.VMEM((2 * FOLD * depth, BATCH), bf16),
                pltpu.VMEM((FOLD * depth, user_count // FOLD), bf16),
                pltpu.VMEM((FOLD * depth, item_count // FOLD), bf16),
                pltpu.VMEM((FOLD * depth, user_count // FOLD), f32),
                pltpu.VMEM((FOLD * depth, item_count // FOLD), f32),
                pltpu.VMEM((2, GROUPS, LANES), f32),
                pltpu.VMEM((2, ranks - 1, GROUPS, LANES), f32),
                pltpu.VMEM((GROUPS, LANES), f32),
                pltpu.SemaphoreType.DMA((2, ranks - 1)),
                pltpu.SemaphoreType.DMA((2, ranks - 1)),
                pltpu.SemaphoreType.DMA((strata,)),
                pltpu.SemaphoreType.DMA((strata,)),
                pltpu.SemaphoreType.DMA((strata, user_count // CHUNK)),
                pltpu.SemaphoreType.DMA((strata, user_count // CHUNK)),
                pltpu.SemaphoreType.DMA((6,)),
            ],
            compiler_params=pltpu.CompilerParams(
                collective_id=0, has_side_effects=True, vmem_limit_bytes=60 * 1024 * 1024
            ),
        )(user_factors, item_factors, tile_rows, tile_cols, tile_vals, tile_count)
        return pl.pallas_call(
            hand_over,
            out_shape=(
                jax.ShapeDtypeStruct((depth, user_count), f32),
                jax.ShapeDtypeStruct((depth, item_count), f32),
            ),
            in_specs=[vmem, vmem],
            out_specs=[pl.BlockSpec(memory_space=pl.ANY)] * 2,
            scratch_shapes=[pltpu.SemaphoreType.DMA((2,))],
        )(*[pltpu.with_memory_space_constraint(x, pltpu.VMEM) for x in moved])

    placed = (
        P("rank", "blk"),
        P("rank", "blk"),
        P("blk", None, None),
        P("blk", None, None),
        P("blk", None, None),
        P("blk", None),
    )
    return jax.shard_map(
        per_device,
        mesh=mesh,
        in_specs=placed,
        out_specs=(P("rank", "blk"), P("rank", "blk")),
        check_vma=False,
    )
```

```python
import functools

import jax
import jax.numpy as jnp
from jax import lax
from jax.experimental import pallas as pl
from jax.experimental.pallas import tpu as pltpu
from jax.sharding import PartitionSpec as P

BATCH = 1024
LANES = 128
GROUPS = BATCH // LANES
CHUNK = 256
PACK = 16
FOLD = 2
LEARN_RATE = 0.05
DECAY_WEIGHT = 0.02
MESH = pl.DeviceIdType.MESH


def split_rows(block):
    high = block.astype(jnp.bfloat16)
    low = (block - high.astype(jnp.float32)).astype(jnp.bfloat16)
    return high, low


def kernel(
    blocks, ranks,
    u_in, v_in, rows_in, cols_in, vals_in, count_in,
    u_out, v_out,
    rows, cols, vals, count, users, u_cat, v_cat, held, tiles, chooser, sides, spreader, u_pick, v_pick,
    u_step, v_step, u_turn, v_turn, u_moved, v_moved,
    partial, arrived, errs,
    part_send, part_recv, tile_send, tile_recv, user_send, user_recv, load_sem,
):
    depth, user_count = u_in.shape
    item_count = v_in.shape[1]
    strata, tile = rows_in.shape[1:]
    per_tile = tile // BATCH
    spans = tile // LANES
    user_keys = user_count // FOLD
    item_keys = item_count // FOLD
    blk = lax.axis_index("blk")
    rank = lax.axis_index("rank")

    def at_blk(shift):
        return (lax.rem(blk + (shift % blocks), blocks), rank)

    def at_rank(shift):
        return (blk, lax.rem(rank + (shift % ranks), ranks))

    loads = [
        pltpu.make_async_copy(source, target, load_sem.at[i])
        for i, (source, target) in enumerate(
            (
                (count_in, count), (rows_in, rows), (cols_in, cols), (vals_in, vals),
                (u_in, users.at[0]), (v_in, v_out),
            )
        )
    ]
    for load in loads:
        load.start()
    barrier = pltpu.get_barrier_semaphore()
    met = [at_rank(o) for o in range(1, ranks)]
    met += [at_blk(o) for o in range(1, strata)] + [at_blk(-o) for o in range(1, strata)]
    for device in met:
        pl.semaphore_signal(barrier, inc=1, device_id=device, device_id_type=MESH)
    for i in (0, 1, 2, 4, 5):
        loads[i].wait()

    stratum_at = lax.broadcasted_iota(jnp.int32, (strata, LANES), 0)
    lane_at = lax.broadcasted_iota(jnp.int32, (strata, LANES), 1)
    live = jnp.zeros((strata, LANES), jnp.int32)
    for s in range(strata):
        live = jnp.where(stratum_at == s, count[0, s], live)

    def hold_places(first, last):
        for r in range(first, last):
            here = slice(r * LANES, (r + 1) * LANES)
            alive = lane_at + r * LANES < live
            held[:, r, :] = jnp.where(alive, rows[0, :, here], -1).astype(jnp.float32)
            held[:, spans + r, :] = jnp.where(alive, cols[0, :, here], -1).astype(jnp.float32)

    hold_places(0, GROUPS)
    for first in (0, spans):
        tiles[0, first : first + GROUPS] = held[0, first : first + GROUPS]

    parts = ((0, user_count, 0), (user_count, item_count, spans))
    down = lax.broadcasted_iota(jnp.int16, (PACK, LANES), 0)
    across = lax.broadcasted_iota(jnp.int32, (LANES, LANES), 1)
    ones = jnp.ones((PACK, LANES), jnp.bfloat16)
    zeros = jnp.zeros((PACK, LANES), jnp.bfloat16)

    def index_of(s, q, first):
        at = pl.multiple_of(first + q * GROUPS, GROUPS)
        return tiles[s, pl.ds(at, GROUPS), :].astype(jnp.int32)

    folded = ((0, user_keys, 0, 0), (1, item_keys, spans, user_keys))

    def build_chooser(slot, s, q, wanted=folded):
        for p, size, first, base in wanted:
            index = index_of(s, q, first)
            side = index >= size
            sides[slot, p] = jnp.where(side, 1.0, 0.0)
            index = jnp.where(side, index - size, index)
            for j in range(GROUPS):
                row = jnp.broadcast_to(index[j : j + 1, :], (PACK, LANES)).astype(jnp.int16)
                for t in range(base, base + size, PACK):
                    chooser[t : t + PACK, j * LANES : (j + 1) * LANES] = jnp.where(down == row, ones, zeros)
                    row = row - jnp.int16(PACK)

    def build_spreader(s, q):
        for p, size, first, base in folded:
            index = index_of(s, q, first)
            index = jnp.transpose(jnp.where(index >= size, index - size, index))
            for j in range(GROUPS):
                column = jnp.broadcast_to(index[:, j : j + 1], (LANES, LANES))
                for t in range(0, size, LANES):
                    spreader[j * LANES : (j + 1) * LANES, base + t : base + t + LANES] = (
                        jnp.where(across + t == column, 1.0, 0.0).astype(jnp.bfloat16)
                    )

    def fold(cat, t, pieces):
        keys = cat.shape[1]
        b, at = t // keys, t % keys
        for i, piece in enumerate(pieces):
            row = (b * len(pieces) + i) * depth
            cat[row : row + depth, at : at + CHUNK] = piece

    def cut_users(s, t):
        fold(u_cat, t, split_rows(users[s, :, t : t + CHUNK]))

    def cut_items():
        for t in range(0, item_count, CHUNK):
            fold(v_cat, t, split_rows(v_out[:, t : t + CHUNK]))

    def tile_copy(s):
        return pltpu.make_async_remote_copy(
            src_ref=held.at[s], dst_ref=tiles.at[s],
            send_sem=tile_send.at[s], recv_sem=tile_recv.at[s],
            device_id=(lax.rem(blk + blocks - s, blocks), rank),
            device_id_type=MESH,
        )

    def user_copy(s, t):
        here = slice(t, t + CHUNK)
        return pltpu.make_async_remote_copy(
            src_ref=users.at[s, :, here], dst_ref=users.at[s + 1, :, here],
            send_sem=user_send.at[s, t // CHUNK], recv_sem=user_recv.at[s, t // CHUNK],
            device_id=at_blk(-1), device_id_type=MESH,
        )

    def home(t):
        here = slice(t, t + CHUNK)
        return pltpu.make_async_remote_copy(
            src_ref=users.at[strata - 1, :, here], dst_ref=u_out.at[:, here],
            send_sem=user_send.at[strata - 1, t // CHUNK], recv_sem=user_recv.at[strata - 1, t // CHUNK],
            device_id=at_blk(strata - 1), device_id_type=MESH,
        )

    def part_copy(slot, o):
        return pltpu.make_async_remote_copy(
            src_ref=partial.at[slot], dst_ref=arrived.at[slot, o - 1],
            send_sem=part_send.at[slot, o - 1], recv_sem=part_recv.at[slot, o - 1],
            device_id=at_rank(o), device_id_type=MESH,
        )

    group_at = lax.broadcasted_iota(jnp.int32, (GROUPS, LANES), 0)

    user_rows, item_rows = slice(0, user_keys), slice(user_keys, user_keys + item_keys)

    def side_of(slot, p, j):
        return jnp.broadcast_to(sides[slot, p, j : j + 1, :], (depth, LANES))

    def pick(cat, slot, p, c):
        rows = (user_rows, item_rows)[p]
        both = jnp.dot(cat[...], chooser[rows, c : c + CHUNK], preferred_element_type=jnp.float32)
        found = []
        for g in range(0, CHUNK, LANES):
            at = both[:, g : g + LANES]
            half = at.shape[0] // 2
            first, second = at[:half], at[half:]
            if half > depth:
                first, second = first[:depth] + first[depth:], second[:depth] + second[depth:]
            found.append(jnp.where(side_of(slot, p, (c + g) // LANES) > 0.5, second, first))
        return found

    def pick_whole(cat, slot, p, target, c):
        for g, found in enumerate(pick(cat, slot, p, c)):
            target[slot, :, c + g * LANES : c + (g + 1) * LANES] = found

    def pick_moved(turned, slot, p, target, c):
        for g, found in enumerate(pick(turned, slot, p, c)):
            here = slice(c + g * LANES, c + (g + 1) * LANES)
            target[slot, :, here] += found

    def sum_parts(slot, pick_last):
        total = jnp.zeros((GROUPS, LANES), jnp.float32)
        for c in range(0, BATCH, CHUNK):
            pick_last(c)
            for j in range(c // LANES, (c + CHUNK) // LANES):
                here = slice(j * LANES, (j + 1) * LANES)
                sums = jnp.sum(u_pick[slot, :, here] * v_pick[slot, :, here], axis=0, keepdims=True)
                total = jnp.where(group_at == j, sums, total)
        partial[slot] = total

    chunks = range(0, BATCH, CHUNK)

    def send_parts(slot):
        for o in sorted(range(1, ranks), key=lambda o: abs(o - ranks // 2)):
            part_copy(slot, o).start()

    def get_errors(s, q, slot):
        for o in range(1, ranks):
            part_copy(slot, o).wait_recv()
        total = partial[slot]
        for o in range(1, ranks):
            total = total + arrived[slot, o - 1]
        at = pl.multiple_of(2 * spans + q * GROUPS, GROUPS)
        errs[...] = LEARN_RATE * (tiles[s, pl.ds(at, GROUPS), :] - total)

    def make_steps(slot, p, steps, wanted=(0, 1)):
        mine, other = ((u_pick, v_pick), (v_pick, u_pick))[p]
        for j in range(GROUPS):
            here = slice(j * LANES, (j + 1) * LANES)
            e = errs[j : j + 1, :]
            pieces = split_rows(e * other[slot, :, here] - LEARN_RATE * DECAY_WEIGHT * mine[slot, :, here])
            side = side_of(slot, p, j).astype(jnp.bfloat16)
            for w in wanted:
                second = pieces[w] * side
                row = FOLD * depth * w
                steps[row : row + depth, here] = pieces[w] - second
                steps[row + depth : row + 2 * depth, here] = second

    def spread(steps, first):
        return jnp.dot(steps, spreader[:, first : first + CHUNK], preferred_element_type=jnp.float32)

    def add_users(s, t, change):
        for b in range(FOLD):
            here = slice(b * user_keys + t, b * user_keys + t + CHUNK)
            users[s, :, here] += change[b * depth : (b + 1) * depth]

    def add_items(t, change):
        for b in range(FOLD):
            here = slice(b * item_keys + t, b * item_keys + t + CHUNK)
            v_out[:, here] += change[b * depth : (b + 1) * depth]

    highs, lows = slice(0, FOLD * depth), slice(FOLD * depth, 2 * FOLD * depth)

    def spread_both(steps, first):
        change = spread(steps[...], first)
        return change[highs] + change[lows]

    def turn_part(steps, base, t, moved, turned):
        change = spread(steps[highs], base + t)
        moved[:, t : t + CHUNK] = change
        turned[:, t : t + CHUNK] = change.astype(jnp.bfloat16)

    for t in range(0, user_count, CHUNK):
        cut_users(0, t)
    build_chooser(0, 0, 0, folded[:1])
    for c in chunks:
        pick_whole(u_cat, 0, 0, u_pick, c)
    cut_items()
    build_chooser(0, 0, 0, folded[1:])
    sum_parts(0, lambda c: pick_whole(v_cat, 0, 1, v_pick, c))
    pl.semaphore_wait(barrier, len(met))
    send_parts(0)
    hold_places(GROUPS, spans)
    loads[3].wait()
    for r in range(spans):
        held[:, 2 * spans + r, :] = vals[0, :, r * LANES : (r + 1) * LANES]
    tiles[0] = held[0]
    for s in range(1, strata):
        tile_copy(s).start()

    @pl.loop(0, strata)
    def _(s):
        @pl.loop(0, per_tile - 1)
        def _(q):
            slot = (s * per_tile + q) % 2
            build_chooser(1 - slot, s, q + 1)
            for c in chunks:
                pick_whole(u_cat, 1 - slot, 0, u_pick, c)
                pick_whole(v_cat, 1 - slot, 1, v_pick, c)
            build_spreader(s, q)
            get_errors(s, q, slot)
            make_steps(slot, 1, v_step, (0,))
            for t in range(0, item_keys, CHUNK):
                turn_part(v_step, user_keys, t, v_moved, v_turn)
            make_steps(slot, 0, u_step, (0,))
            for t in range(0, user_keys, CHUNK):
                turn_part(u_step, 0, t, u_moved, u_turn)
            for c in chunks:
                pick_moved(v_turn, 1 - slot, 1, v_pick, c)
            sum_parts(1 - slot, lambda c: pick_moved(u_turn, 1 - slot, 0, u_pick, c))
            send_parts(1 - slot)
            make_steps(slot, 0, u_step, (1,))
            make_steps(slot, 1, v_step, (1,))
            for t in range(0, user_keys, CHUNK):
                add_users(s, t, u_moved[:, t : t + CHUNK] + spread(u_step[lows], t))
            for t in range(0, user_count, CHUNK):
                cut_users(s, t)
            for t in range(0, item_keys, CHUNK):
                add_items(t, v_moved[:, t : t + CHUNK] + spread(v_step[lows], user_keys + t))
            cut_items()
            for o in range(1, ranks):
                part_copy(slot, o).wait_send()

        q = per_tile - 1
        slot = (s * per_tile + q) % 2
        build_spreader(s, q)

        @pl.when(s < strata - 1)
        def _():
            tile_copy(s + 1).wait_recv()
            build_chooser(1 - slot, s + 1, 0)

        get_errors(s, q, slot)
        make_steps(slot, 0, u_step)
        for t in range(0, user_keys, CHUNK):
            add_users(s, t, spread_both(u_step, t))

        @pl.when(s < strata - 1)
        def _():
            for t in range(0, user_count, CHUNK):
                user_copy(s, t).start()

        @pl.when(s == strata - 1)
        def _():
            for t in range(0, user_count, CHUNK):
                home(t).start()

        make_steps(slot, 1, v_step)
        for t in range(0, item_keys, CHUNK):
            add_items(t, spread_both(v_step, user_keys + t))
        for o in range(1, ranks):
            part_copy(slot, o).wait_send()

        @pl.when(s < strata - 1)
        def _():
            cut_items()
            for c in chunks:
                pick_whole(v_cat, 1 - slot, 1, v_pick, c)
            for t in range(0, user_count, CHUNK):
                user_copy(s, t).wait()
                cut_users(s + 1, t)
            sum_parts(1 - slot, lambda c: pick_whole(u_cat, 1 - slot, 0, u_pick, c))
            send_parts(1 - slot)

    for s in range(1, strata):
        tile_copy(s).wait_send()
    for t in range(0, user_count, CHUNK):
        home(t).wait()


def hand_over(u_in, v_in, u_out, v_out, sem):
    copies = [
        pltpu.make_async_copy(source, target, sem.at[i])
        for i, (source, target) in enumerate(((v_in, v_out), (u_in, u_out)))
    ]
    for copy in copies:
        copy.start()
    for copy in copies:
        copy.wait()


def solution(mesh):
    blocks, ranks = mesh.shape["blk"], mesh.shape["rank"]

    def per_device(user_factors, item_factors, tile_rows, tile_cols, tile_vals, tile_count):
        depth, user_count = user_factors.shape
        item_count = item_factors.shape[1]
        strata, tile = tile_rows.shape[1:]
        held = (strata, 3 * tile // LANES, LANES)
        vmem = pl.BlockSpec(memory_space=pltpu.VMEM)
        f32, bf16 = jnp.float32, jnp.bfloat16
        moved = pl.pallas_call(
            functools.partial(kernel, blocks, ranks),
            out_shape=(
                pltpu.VMEM((depth, user_count), f32),
                pltpu.VMEM((depth, item_count), f32),
            ),
            in_specs=[pl.BlockSpec(memory_space=pl.ANY)] * 6,
            out_specs=(vmem, vmem),
            scratch_shapes=[
                pltpu.VMEM(tile_rows.shape, jnp.int32),
                pltpu.VMEM(tile_cols.shape, jnp.int32),
                pltpu.VMEM(tile_vals.shape, f32),
                pltpu.SMEM(tile_count.shape, jnp.int32),
                pltpu.VMEM((strata, depth, user_count), f32),
                pltpu.VMEM((2 * FOLD * depth, user_count // FOLD), bf16),
                pltpu.VMEM((2 * FOLD * depth, item_count // FOLD), bf16),
                pltpu.VMEM(held, f32),
                pltpu.VMEM(held, f32),
                pltpu.VMEM(((user_count + item_count) // FOLD, BATCH), bf16),
                pltpu.VMEM((2, 2, GROUPS, LANES), f32),
                pltpu.VMEM((BATCH, (user_count + item_count) // FOLD), bf16),
                pltpu.VMEM((2, depth, BATCH), f32),
                pltpu.VMEM((2, depth, BATCH), f32),
                pltpu.VMEM((2 * FOLD * depth, BATCH), bf16),
                pltpu.VMEM((2 * FOLD * depth, BATCH), bf16),
                pltpu.VMEM((FOLD * depth, user_count // FOLD), bf16),
                pltpu.VMEM((FOLD * depth, item_count // FOLD), bf16),
                pltpu.VMEM((FOLD * depth, user_count // FOLD), f32),
                pltpu.VMEM((FOLD * depth, item_count // FOLD), f32),
                pltpu.VMEM((2, GROUPS, LANES), f32),
                pltpu.VMEM((2, ranks - 1, GROUPS, LANES), f32),
                pltpu.VMEM((GROUPS, LANES), f32),
                pltpu.SemaphoreType.DMA((2, ranks - 1)),
                pltpu.SemaphoreType.DMA((2, ranks - 1)),
                pltpu.SemaphoreType.DMA((strata,)),
                pltpu.SemaphoreType.DMA((strata,)),
                pltpu.SemaphoreType.DMA((strata, user_count // CHUNK)),
                pltpu.SemaphoreType.DMA((strata, user_count // CHUNK)),
                pltpu.SemaphoreType.DMA((6,)),
            ],
            compiler_params=pltpu.CompilerParams(
                collective_id=0, has_side_effects=True, vmem_limit_bytes=60 * 1024 * 1024
            ),
        )(user_factors, item_factors, tile_rows, tile_cols, tile_vals, tile_count)
        return pl.pallas_call(
            hand_over,
            out_shape=(
                jax.ShapeDtypeStruct((depth, user_count), f32),
                jax.ShapeDtypeStruct((depth, item_count), f32),
            ),
            in_specs=[vmem, vmem],
            out_specs=[pl.BlockSpec(memory_space=pl.ANY)] * 2,
            scratch_shapes=[pltpu.SemaphoreType.DMA((2,))],
        )(*[pltpu.with_memory_space_constraint(x, pltpu.VMEM) for x in moved])

    placed = (
        P("rank", "blk"),
        P("rank", "blk"),
        P("blk", None, None),
        P("blk", None, None),
        P("blk", None, None),
        P("blk", None),
    )
    return jax.shard_map(
        per_device,
        mesh=mesh,
        in_specs=placed,
        out_specs=(P("rank", "blk"), P("rank", "blk")),
        check_vma=False,
    )
```

```python
import functools

import jax
import jax.numpy as jnp
from jax import lax
from jax.experimental import pallas as pl
from jax.experimental.pallas import tpu as pltpu
from jax.sharding import PartitionSpec as P

BATCH = 1024
LANES = 128
GROUPS = BATCH // LANES
CHUNK = 256
PACK = 16
FOLD = 2
LEARN_RATE = 0.05
DECAY_WEIGHT = 0.02
MESH = pl.DeviceIdType.MESH


def split_rows(block):
    high = block.astype(jnp.bfloat16)
    low = (block - high.astype(jnp.float32)).astype(jnp.bfloat16)
    return high, low


def kernel(
    blocks, ranks,
    u_in, v_in, rows_in, cols_in, vals_in, count_in,
    u_out, v_out,
    rows, cols, vals, count, users, u_cat, v_cat, held, tiles, chooser, sides, spreader, u_pick, v_pick,
    u_step, v_step, u_turn, v_turn, u_moved, v_moved,
    partial, arrived, errs,
    part_send, part_recv, tile_send, tile_recv, user_send, user_recv, load_sem,
):
    depth, user_count = u_in.shape
    item_count = v_in.shape[1]
    strata, tile = rows_in.shape[1:]
    per_tile = tile // BATCH
    spans = tile // LANES
    user_keys = user_count // FOLD
    item_keys = item_count // FOLD
    blk = lax.axis_index("blk")
    rank = lax.axis_index("rank")

    def at_blk(shift):
        return (lax.rem(blk + (shift % blocks), blocks), rank)

    def at_rank(shift):
        return (blk, lax.rem(rank + (shift % ranks), ranks))

    loads = [
        pltpu.make_async_copy(source, target, load_sem.at[i])
        for i, (source, target) in enumerate(
            (
                (count_in, count), (rows_in, rows), (cols_in, cols), (vals_in, vals),
                (u_in, users.at[0]), (v_in, v_out),
            )
        )
    ]
    for load in loads:
        load.start()
    barrier = pltpu.get_barrier_semaphore()
    met = [at_rank(o) for o in range(1, ranks)]
    met += [at_blk(o) for o in range(1, strata)] + [at_blk(-o) for o in range(1, strata)]
    for device in met:
        pl.semaphore_signal(barrier, inc=1, device_id=device, device_id_type=MESH)
    for i in (0, 1, 2, 4, 5):
        loads[i].wait()

    stratum_at = lax.broadcasted_iota(jnp.int32, (strata, LANES), 0)
    lane_at = lax.broadcasted_iota(jnp.int32, (strata, LANES), 1)
    live = jnp.zeros((strata, LANES), jnp.int32)
    for s in range(strata):
        live = jnp.where(stratum_at == s, count[0, s], live)

    def hold_places(first, last):
        for r in range(first, last):
            here = slice(r * LANES, (r + 1) * LANES)
            alive = lane_at + r * LANES < live
            held[:, r, :] = jnp.where(alive, rows[0, :, here], -1).astype(jnp.float32)
            held[:, spans + r, :] = jnp.where(alive, cols[0, :, here], -1).astype(jnp.float32)

    hold_places(0, GROUPS)
    for first in (0, spans):
        tiles[0, first : first + GROUPS] = held[0, first : first + GROUPS]

    parts = ((0, user_count, 0), (user_count, item_count, spans))
    down = lax.broadcasted_iota(jnp.int16, (PACK, LANES), 0)
    across = lax.broadcasted_iota(jnp.int32, (LANES, LANES), 1)
    ones = jnp.ones((PACK, LANES), jnp.bfloat16)
    zeros = jnp.zeros((PACK, LANES), jnp.bfloat16)

    def index_of(s, q, first):
        at = pl.multiple_of(first + q * GROUPS, GROUPS)
        return tiles[s, pl.ds(at, GROUPS), :].astype(jnp.int32)

    folded = ((0, user_keys, 0, 0), (1, item_keys, spans, user_keys))

    def build_chooser(slot, s, q, wanted=folded):
        for p, size, first, base in wanted:
            index = index_of(s, q, first)
            side = index >= size
            sides[slot, p] = jnp.where(side, 1.0, 0.0)
            index = jnp.where(side, index - size, index)
            for j in range(GROUPS):
                row = jnp.broadcast_to(index[j : j + 1, :], (PACK, LANES)).astype(jnp.int16)
                for t in range(base, base + size, PACK):
                    chooser[t : t + PACK, j * LANES : (j + 1) * LANES] = jnp.where(down == row, ones, zeros)
                    row = row - jnp.int16(PACK)

    def build_spreader(s, q):
        for p, size, first, base in folded:
            index = index_of(s, q, first)
            index = jnp.transpose(jnp.where(index >= size, index - size, index))
            for j in range(GROUPS):
                column = jnp.broadcast_to(index[:, j : j + 1], (LANES, LANES))
                for t in range(0, size, LANES):
                    spreader[j * LANES : (j + 1) * LANES, base + t : base + t + LANES] = (
                        jnp.where(across + t == column, 1.0, 0.0).astype(jnp.bfloat16)
                    )

    def fold(cat, t, pieces):
        keys = cat.shape[1]
        b, at = t // keys, t % keys
        for i, piece in enumerate(pieces):
            row = (b * len(pieces) + i) * depth
            cat[row : row + depth, at : at + CHUNK] = piece

    def cut_users(s, t):
        fold(u_cat, t, split_rows(users[s, :, t : t + CHUNK]))

    def cut_items():
        for t in range(0, item_count, CHUNK):
            fold(v_cat, t, split_rows(v_out[:, t : t + CHUNK]))

    def tile_copy(s):
        return pltpu.make_async_remote_copy(
            src_ref=held.at[s], dst_ref=tiles.at[s],
            send_sem=tile_send.at[s], recv_sem=tile_recv.at[s],
            device_id=(lax.rem(blk + blocks - s, blocks), rank),
            device_id_type=MESH,
        )

    def user_copy(s, t):
        here = slice(t, t + CHUNK)
        return pltpu.make_async_remote_copy(
            src_ref=users.at[s, :, here], dst_ref=users.at[s + 1, :, here],
            send_sem=user_send.at[s, t // CHUNK], recv_sem=user_recv.at[s, t // CHUNK],
            device_id=(lax.rem(blk + blocks - 1 + s // (strata - 1) * strata, blocks), rank),
            device_id_type=MESH,
        )

    def part_copy(slot, o):
        return pltpu.make_async_remote_copy(
            src_ref=partial.at[slot], dst_ref=arrived.at[slot, o - 1],
            send_sem=part_send.at[slot, o - 1], recv_sem=part_recv.at[slot, o - 1],
            device_id=at_rank(o), device_id_type=MESH,
        )

    group_at = lax.broadcasted_iota(jnp.int32, (GROUPS, LANES), 0)

    user_rows, item_rows = slice(0, user_keys), slice(user_keys, user_keys + item_keys)

    def side_of(slot, p, j):
        return jnp.broadcast_to(sides[slot, p, j : j + 1, :], (depth, LANES))

    def pick(cat, slot, p, c):
        rows = (user_rows, item_rows)[p]
        both = jnp.dot(cat[...], chooser[rows, c : c + CHUNK], preferred_element_type=jnp.float32)
        found = []
        for g in range(0, CHUNK, LANES):
            at = both[:, g : g + LANES]
            half = at.shape[0] // 2
            first, second = at[:half], at[half:]
            if half > depth:
                first, second = first[:depth] + first[depth:], second[:depth] + second[depth:]
            found.append(jnp.where(side_of(slot, p, (c + g) // LANES) > 0.5, second, first))
        return found

    def pick_half(b, c):
        rows = slice(2 * b * depth, 2 * (b + 1) * depth)
        both = jnp.dot(
            u_cat[rows, :], chooser[user_rows, c : c + CHUNK], preferred_element_type=jnp.float32
        )
        return both[:depth] + both[depth:]

    def pick_whole(cat, slot, p, target, c):
        for g, found in enumerate(pick(cat, slot, p, c)):
            target[slot, :, c + g * LANES : c + (g + 1) * LANES] = found

    def pick_moved(turned, slot, p, target, c):
        for g, found in enumerate(pick(turned, slot, p, c)):
            here = slice(c + g * LANES, c + (g + 1) * LANES)
            target[slot, :, here] += found

    def sum_parts(slot, pick_last):
        total = jnp.zeros((GROUPS, LANES), jnp.float32)
        for c in range(0, BATCH, CHUNK):
            pick_last(c)
            for j in range(c // LANES, (c + CHUNK) // LANES):
                here = slice(j * LANES, (j + 1) * LANES)
                sums = jnp.sum(u_pick[slot, :, here] * v_pick[slot, :, here], axis=0, keepdims=True)
                total = jnp.where(group_at == j, sums, total)
        partial[slot] = total

    chunks = range(0, BATCH, CHUNK)

    def send_parts(slot):
        for o in sorted(range(1, ranks), key=lambda o: abs(o - ranks // 2)):
            part_copy(slot, o).start()

    def get_errors(s, q, slot):
        for o in range(1, ranks):
            part_copy(slot, o).wait_recv()
        total = partial[slot]
        for o in range(1, ranks):
            total = total + arrived[slot, o - 1]
        at = pl.multiple_of(2 * spans + q * GROUPS, GROUPS)
        errs[...] = LEARN_RATE * (tiles[s, pl.ds(at, GROUPS), :] - total)

    def make_steps(slot, p, steps, wanted=(0, 1)):
        mine, other = ((u_pick, v_pick), (v_pick, u_pick))[p]
        for j in range(GROUPS):
            here = slice(j * LANES, (j + 1) * LANES)
            e = errs[j : j + 1, :]
            pieces = split_rows(e * other[slot, :, here] - LEARN_RATE * DECAY_WEIGHT * mine[slot, :, here])
            side = side_of(slot, p, j).astype(jnp.bfloat16)
            for w in wanted:
                second = pieces[w] * side
                row = FOLD * depth * w
                steps[row : row + depth, here] = pieces[w] - second
                steps[row + depth : row + 2 * depth, here] = second

    def spread(steps, first):
        return jnp.dot(steps, spreader[:, first : first + CHUNK], preferred_element_type=jnp.float32)

    def add_users(s, t, change):
        for b in range(FOLD):
            here = slice(b * user_keys + t, b * user_keys + t + CHUNK)
            users[s, :, here] += change[b * depth : (b + 1) * depth]

    def add_items(t, change):
        for b in range(FOLD):
            here = slice(b * item_keys + t, b * item_keys + t + CHUNK)
            v_out[:, here] += change[b * depth : (b + 1) * depth]

    highs, lows = slice(0, FOLD * depth), slice(FOLD * depth, 2 * FOLD * depth)

    def spread_both(steps, first):
        change = spread(steps[...], first)
        return change[highs] + change[lows]

    def turn_part(steps, base, t, moved, turned):
        change = spread(steps[highs], base + t)
        moved[:, t : t + CHUNK] = change
        turned[:, t : t + CHUNK] = change.astype(jnp.bfloat16)

    for t in range(0, user_count, CHUNK):
        cut_users(0, t)
    build_chooser(0, 0, 0, folded[:1])
    for c in chunks:
        pick_whole(u_cat, 0, 0, u_pick, c)
    cut_items()
    build_chooser(0, 0, 0, folded[1:])
    sum_parts(0, lambda c: pick_whole(v_cat, 0, 1, v_pick, c))
    pl.semaphore_wait(barrier, len(met))
    send_parts(0)
    hold_places(GROUPS, spans)
    loads[3].wait()
    for r in range(spans):
        held[:, 2 * spans + r, :] = vals[0, :, r * LANES : (r + 1) * LANES]
    tiles[0] = held[0]
    for s in range(1, strata):
        tile_copy(s).start()

    @pl.loop(0, strata)
    def _(s):
        @pl.loop(0, per_tile - 1)
        def _(q):
            slot = (s * per_tile + q) % 2
            build_chooser(1 - slot, s, q + 1)
            for c in chunks:
                pick_whole(u_cat, 1 - slot, 0, u_pick, c)
                pick_whole(v_cat, 1 - slot, 1, v_pick, c)
            build_spreader(s, q)
            get_errors(s, q, slot)
            make_steps(slot, 1, v_step, (0,))
            for t in range(0, item_keys, CHUNK):
                turn_part(v_step, user_keys, t, v_moved, v_turn)
            make_steps(slot, 0, u_step, (0,))
            for t in range(0, user_keys, CHUNK):
                turn_part(u_step, 0, t, u_moved, u_turn)
            for c in chunks:
                pick_moved(v_turn, 1 - slot, 1, v_pick, c)
            sum_parts(1 - slot, lambda c: pick_moved(u_turn, 1 - slot, 0, u_pick, c))
            send_parts(1 - slot)
            make_steps(slot, 0, u_step, (1,))
            make_steps(slot, 1, v_step, (1,))
            for t in range(0, user_keys, CHUNK):
                add_users(s, t, u_moved[:, t : t + CHUNK] + spread(u_step[lows], t))
            for t in range(0, user_count, CHUNK):
                cut_users(s, t)
            for t in range(0, item_keys, CHUNK):
                add_items(t, v_moved[:, t : t + CHUNK] + spread(v_step[lows], user_keys + t))
            cut_items()
            for o in range(1, ranks):
                part_copy(slot, o).wait_send()

        q = per_tile - 1
        slot = (s * per_tile + q) % 2
        build_spreader(s, q)

        @pl.when(s < strata - 1)
        def _():
            tile_copy(s + 1).wait_recv()
            build_chooser(1 - slot, s + 1, 0)

        get_errors(s, q, slot)
        make_steps(slot, 0, u_step)
        for t in range(0, user_keys, CHUNK):
            add_users(s, t, spread_both(u_step, t))
        for t in range(0, user_count, CHUNK):
            user_copy(s, t).start()
        make_steps(slot, 1, v_step)
        for t in range(0, item_keys, CHUNK):
            add_items(t, spread_both(v_step, user_keys + t))
        for o in range(1, ranks):
            part_copy(slot, o).wait_send()

        @pl.when(s < strata - 1)
        def _():
            cut_items()
            for c in chunks:
                pick_whole(v_cat, 1 - slot, 1, v_pick, c)
            user_copy(s, 0).wait()
            cut_users(s + 1, 0)
            for c in chunks:
                here = slice(c, c + CHUNK)
                u_pick[1 - slot, :, here] = pick_half(0, c)
            for t in range(CHUNK, user_count, CHUNK):
                user_copy(s, t).wait()
                cut_users(s + 1, t)

            def pick_rest(c):
                second = pick_half(1, c)
                for g in range(0, CHUNK, LANES):
                    here = slice(c + g, c + g + LANES)
                    side = side_of(1 - slot, 0, (c + g) // LANES) > 0.5
                    u_pick[1 - slot, :, here] = jnp.where(
                        side, second[:, g : g + LANES], u_pick[1 - slot, :, here]
                    )

            sum_parts(1 - slot, pick_rest)
            send_parts(1 - slot)

    for s in range(1, strata):
        tile_copy(s).wait_send()
    for t in range(0, user_count, CHUNK):
        user_copy(strata - 1, t).wait()
        u_out[:, t : t + CHUNK] = users[strata, :, t : t + CHUNK]


def hand_over(u_in, v_in, u_out, v_out, sem):
    copies = [
        pltpu.make_async_copy(source, target, sem.at[i])
        for i, (source, target) in enumerate(((v_in, v_out), (u_in, u_out)))
    ]
    for copy in copies:
        copy.start()
    for copy in copies:
        copy.wait()


def solution(mesh):
    blocks, ranks = mesh.shape["blk"], mesh.shape["rank"]

    def per_device(user_factors, item_factors, tile_rows, tile_cols, tile_vals, tile_count):
        depth, user_count = user_factors.shape
        item_count = item_factors.shape[1]
        strata, tile = tile_rows.shape[1:]
        held = (strata, 3 * tile // LANES, LANES)
        vmem = pl.BlockSpec(memory_space=pltpu.VMEM)
        f32, bf16 = jnp.float32, jnp.bfloat16
        moved = pl.pallas_call(
            functools.partial(kernel, blocks, ranks),
            out_shape=(
                pltpu.VMEM((depth, user_count), f32),
                pltpu.VMEM((depth, item_count), f32),
            ),
            in_specs=[pl.BlockSpec(memory_space=pl.ANY)] * 6,
            out_specs=(vmem, vmem),
            scratch_shapes=[
                pltpu.VMEM(tile_rows.shape, jnp.int32),
                pltpu.VMEM(tile_cols.shape, jnp.int32),
                pltpu.VMEM(tile_vals.shape, f32),
                pltpu.SMEM(tile_count.shape, jnp.int32),
                pltpu.VMEM((strata + 1, depth, user_count), f32),
                pltpu.VMEM((2 * FOLD * depth, user_count // FOLD), bf16),
                pltpu.VMEM((2 * FOLD * depth, item_count // FOLD), bf16),
                pltpu.VMEM(held, f32),
                pltpu.VMEM(held, f32),
                pltpu.VMEM(((user_count + item_count) // FOLD, BATCH), bf16),
                pltpu.VMEM((2, 2, GROUPS, LANES), f32),
                pltpu.VMEM((BATCH, (user_count + item_count) // FOLD), bf16),
                pltpu.VMEM((2, depth, BATCH), f32),
                pltpu.VMEM((2, depth, BATCH), f32),
                pltpu.VMEM((2 * FOLD * depth, BATCH), bf16),
                pltpu.VMEM((2 * FOLD * depth, BATCH), bf16),
                pltpu.VMEM((FOLD * depth, user_count // FOLD), bf16),
                pltpu.VMEM((FOLD * depth, item_count // FOLD), bf16),
                pltpu.VMEM((FOLD * depth, user_count // FOLD), f32),
                pltpu.VMEM((FOLD * depth, item_count // FOLD), f32),
                pltpu.VMEM((2, GROUPS, LANES), f32),
                pltpu.VMEM((2, ranks - 1, GROUPS, LANES), f32),
                pltpu.VMEM((GROUPS, LANES), f32),
                pltpu.SemaphoreType.DMA((2, ranks - 1)),
                pltpu.SemaphoreType.DMA((2, ranks - 1)),
                pltpu.SemaphoreType.DMA((strata,)),
                pltpu.SemaphoreType.DMA((strata,)),
                pltpu.SemaphoreType.DMA((strata, user_count // CHUNK)),
                pltpu.SemaphoreType.DMA((strata, user_count // CHUNK)),
                pltpu.SemaphoreType.DMA((6,)),
            ],
            compiler_params=pltpu.CompilerParams(
                collective_id=0, has_side_effects=True, vmem_limit_bytes=60 * 1024 * 1024
            ),
        )(user_factors, item_factors, tile_rows, tile_cols, tile_vals, tile_count)
        return pl.pallas_call(
            hand_over,
            out_shape=(
                jax.ShapeDtypeStruct((depth, user_count), f32),
                jax.ShapeDtypeStruct((depth, item_count), f32),
            ),
            in_specs=[vmem, vmem],
            out_specs=[pl.BlockSpec(memory_space=pl.ANY)] * 2,
            scratch_shapes=[pltpu.SemaphoreType.DMA((2,))],
        )(*[pltpu.with_memory_space_constraint(x, pltpu.VMEM) for x in moved])

    placed = (
        P("rank", "blk"),
        P("rank", "blk"),
        P("blk", None, None),
        P("blk", None, None),
        P("blk", None, None),
        P("blk", None),
    )
    return jax.shard_map(
        per_device,
        mesh=mesh,
        in_specs=placed,
        out_specs=(P("rank", "blk"), P("rank", "blk")),
        check_vma=False,
    )
```

```python
import functools

import jax
import jax.numpy as jnp
from jax import lax
from jax.experimental import pallas as pl
from jax.experimental.pallas import tpu as pltpu
from jax.sharding import PartitionSpec as P

BATCH = 1024
LANES = 128
GROUPS = BATCH // LANES
CHUNK = 256
PACK = 16
FOLD = 2
LEARN_RATE = 0.05
DECAY_WEIGHT = 0.02
MESH = pl.DeviceIdType.MESH


def split_rows(block):
    high = block.astype(jnp.bfloat16)
    low = (block - high.astype(jnp.float32)).astype(jnp.bfloat16)
    return high, low


def kernel(
    blocks, ranks,
    u_in, v_in, rows_in, cols_in, vals_in, count_in,
    u_out, v_out,
    rows, cols, vals, count, users, u_cat, v_cat, held, tiles, chooser, sides, spreader, u_pick, v_pick,
    u_step, v_step, u_turn, v_turn, u_moved, v_moved,
    partial, arrived, errs,
    part_send, part_recv, tile_send, tile_recv, user_send, user_recv, load_sem,
):
    depth, user_count = u_in.shape
    item_count = v_in.shape[1]
    strata, tile = rows_in.shape[1:]
    per_tile = tile // BATCH
    spans = tile // LANES
    user_keys = user_count // FOLD
    item_keys = item_count // FOLD
    blk = lax.axis_index("blk")
    rank = lax.axis_index("rank")

    def at_blk(shift):
        return (lax.rem(blk + (shift % blocks), blocks), rank)

    def at_rank(shift):
        return (blk, lax.rem(rank + (shift % ranks), ranks))

    loads = [
        pltpu.make_async_copy(source, target, load_sem.at[i])
        for i, (source, target) in enumerate(
            (
                (count_in, count), (rows_in, rows), (cols_in, cols), (vals_in, vals),
                (u_in, users.at[0]), (v_in, v_out),
            )
        )
    ]
    for load in loads:
        load.start()
    barrier = pltpu.get_barrier_semaphore()
    met = [at_rank(o) for o in range(1, ranks)]
    met += [at_blk(o) for o in range(1, strata)] + [at_blk(-o) for o in range(1, strata)]
    for device in met:
        pl.semaphore_signal(barrier, inc=1, device_id=device, device_id_type=MESH)
    for i in (0, 1, 2, 4, 5):
        loads[i].wait()

    stratum_at = lax.broadcasted_iota(jnp.int32, (strata, LANES), 0)
    lane_at = lax.broadcasted_iota(jnp.int32, (strata, LANES), 1)
    live = jnp.zeros((strata, LANES), jnp.int32)
    for s in range(strata):
        live = jnp.where(stratum_at == s, count[0, s], live)

    def hold_places(first, last):
        for r in range(first, last):
            here = slice(r * LANES, (r + 1) * LANES)
            alive = lane_at + r * LANES < live
            held[:, r, :] = jnp.where(alive, rows[0, :, here], -1).astype(jnp.float32)
            held[:, spans + r, :] = jnp.where(alive, cols[0, :, here], -1).astype(jnp.float32)

    hold_places(0, GROUPS)
    for first in (0, spans):
        tiles[0, first : first + GROUPS] = held[0, first : first + GROUPS]

    parts = ((0, user_count, 0), (user_count, item_count, spans))
    down = lax.broadcasted_iota(jnp.int16, (PACK, LANES), 0)
    across = lax.broadcasted_iota(jnp.int32, (LANES, LANES), 1)
    ones = jnp.ones((PACK, LANES), jnp.bfloat16)
    zeros = jnp.zeros((PACK, LANES), jnp.bfloat16)

    def index_of(s, q, first):
        at = pl.multiple_of(first + q * GROUPS, GROUPS)
        return tiles[s, pl.ds(at, GROUPS), :].astype(jnp.int32)

    folded = ((0, user_keys, 0, 0), (1, item_keys, spans, user_keys))

    def build_chooser(slot, s, q, wanted=folded):
        for p, size, first, base in wanted:
            index = index_of(s, q, first)
            side = index >= size
            sides[slot, p] = jnp.where(side, 1.0, 0.0)
            index = jnp.where(side, index - size, index)
            for j in range(GROUPS):
                row = jnp.broadcast_to(index[j : j + 1, :], (PACK, LANES)).astype(jnp.int16)
                for t in range(base, base + size, PACK):
                    chooser[t : t + PACK, j * LANES : (j + 1) * LANES] = jnp.where(down == row, ones, zeros)
                    row = row - jnp.int16(PACK)

    def build_spreader(s, q):
        for p, size, first, base in folded:
            index = index_of(s, q, first)
            index = jnp.transpose(jnp.where(index >= size, index - size, index))
            for j in range(GROUPS):
                column = jnp.broadcast_to(index[:, j : j + 1], (LANES, LANES))
                for t in range(0, size, LANES):
                    spreader[j * LANES : (j + 1) * LANES, base + t : base + t + LANES] = (
                        jnp.where(across + t == column, 1.0, 0.0).astype(jnp.bfloat16)
                    )

    def fold(cat, t, pieces):
        keys = cat.shape[1]
        b, at = t // keys, t % keys
        for i, piece in enumerate(pieces):
            row = (b * len(pieces) + i) * depth
            cat[row : row + depth, at : at + CHUNK] = piece

    def cut_users(s, t):
        fold(u_cat, t, split_rows(users[s, :, t : t + CHUNK]))

    def cut_items():
        for t in range(0, item_count, CHUNK):
            fold(v_cat, t, split_rows(v_out[:, t : t + CHUNK]))

    def tile_copy(s):
        return pltpu.make_async_remote_copy(
            src_ref=held.at[s], dst_ref=tiles.at[s],
            send_sem=tile_send.at[s], recv_sem=tile_recv.at[s],
            device_id=(lax.rem(blk + blocks - s, blocks), rank),
            device_id_type=MESH,
        )

    def user_copy(s, t):
        here = slice(t, t + CHUNK)
        return pltpu.make_async_remote_copy(
            src_ref=users.at[s, :, here], dst_ref=users.at[s + 1, :, here],
            send_sem=user_send.at[s, t // CHUNK], recv_sem=user_recv.at[s, t // CHUNK],
            device_id=(lax.rem(blk + blocks - 1 + s // (strata - 1) * strata, blocks), rank),
            device_id_type=MESH,
        )

    def part_copy(slot, o):
        return pltpu.make_async_remote_copy(
            src_ref=partial.at[slot], dst_ref=arrived.at[slot, o - 1],
            send_sem=part_send.at[slot, o - 1], recv_sem=part_recv.at[slot, o - 1],
            device_id=at_rank(o), device_id_type=MESH,
        )

    group_at = lax.broadcasted_iota(jnp.int32, (GROUPS, LANES), 0)

    user_rows, item_rows = slice(0, user_keys), slice(user_keys, user_keys + item_keys)

    def side_of(slot, p, j):
        return jnp.broadcast_to(sides[slot, p, j : j + 1, :], (depth, LANES))

    def pick(cat, slot, p, c):
        rows = (user_rows, item_rows)[p]
        both = jnp.dot(cat[...], chooser[rows, c : c + CHUNK], preferred_element_type=jnp.float32)
        found = []
        for g in range(0, CHUNK, LANES):
            at = both[:, g : g + LANES]
            half = at.shape[0] // 2
            first, second = at[:half], at[half:]
            if half > depth:
                first, second = first[:depth] + first[depth:], second[:depth] + second[depth:]
            found.append(jnp.where(side_of(slot, p, (c + g) // LANES) > 0.5, second, first))
        return found

    def pick_half(b, c):
        rows = slice(2 * b * depth, 2 * (b + 1) * depth)
        both = jnp.dot(
            u_cat[rows, :], chooser[user_rows, c : c + CHUNK], preferred_element_type=jnp.float32
        )
        return both[:depth] + both[depth:]

    def pick_whole(cat, slot, p, target, c):
        for g, found in enumerate(pick(cat, slot, p, c)):
            target[slot, :, c + g * LANES : c + (g + 1) * LANES] = found

    def pick_moved(turned, slot, p, target, c):
        for g, found in enumerate(pick(turned, slot, p, c)):
            here = slice(c + g * LANES, c + (g + 1) * LANES)
            target[slot, :, here] += found

    def sum_parts(slot, pick_last):
        total = jnp.zeros((GROUPS, LANES), jnp.float32)
        for c in range(0, BATCH, CHUNK):
            pick_last(c)
            for j in range(c // LANES, (c + CHUNK) // LANES):
                here = slice(j * LANES, (j + 1) * LANES)
                sums = jnp.sum(u_pick[slot, :, here] * v_pick[slot, :, here], axis=0, keepdims=True)
                total = jnp.where(group_at == j, sums, total)
        partial[slot] = total

    chunks = range(0, BATCH, CHUNK)

    def send_parts(slot):
        for o in sorted(range(1, ranks), key=lambda o: abs(o - ranks // 2)):
            part_copy(slot, o).start()

    def get_errors(s, q, slot):
        for o in range(1, ranks):
            part_copy(slot, o).wait_recv()
        total = partial[slot]
        for o in range(1, ranks):
            total = total + arrived[slot, o - 1]
        at = pl.multiple_of(2 * spans + q * GROUPS, GROUPS)
        errs[...] = LEARN_RATE * (tiles[s, pl.ds(at, GROUPS), :] - total)

    def make_steps(slot, p, steps, wanted=(0, 1)):
        mine, other = ((u_pick, v_pick), (v_pick, u_pick))[p]
        for j in range(GROUPS):
            here = slice(j * LANES, (j + 1) * LANES)
            e = errs[j : j + 1, :]
            pieces = split_rows(e * other[slot, :, here] - LEARN_RATE * DECAY_WEIGHT * mine[slot, :, here])
            side = side_of(slot, p, j).astype(jnp.bfloat16)
            for w in wanted:
                second = pieces[w] * side
                row = FOLD * depth * w
                steps[row : row + depth, here] = pieces[w] - second
                steps[row + depth : row + 2 * depth, here] = second

    def spread(steps, first):
        return jnp.dot(steps, spreader[:, first : first + CHUNK], preferred_element_type=jnp.float32)

    def add_users(s, t, change):
        for b in range(FOLD):
            here = slice(b * user_keys + t, b * user_keys + t + CHUNK)
            users[s, :, here] += change[b * depth : (b + 1) * depth]

    def add_items(t, change):
        for b in range(FOLD):
            here = slice(b * item_keys + t, b * item_keys + t + CHUNK)
            v_out[:, here] += change[b * depth : (b + 1) * depth]

    highs, lows = slice(0, FOLD * depth), slice(FOLD * depth, 2 * FOLD * depth)

    def spread_both(steps, first):
        change = spread(steps[...], first)
        return change[highs] + change[lows]

    def turn_part(steps, base, t, moved, turned):
        change = spread(steps[highs], base + t)
        moved[:, t : t + CHUNK] = change
        turned[:, t : t + CHUNK] = change.astype(jnp.bfloat16)

    for t in range(0, user_count, CHUNK):
        cut_users(0, t)
    build_chooser(0, 0, 0, folded[:1])
    for c in chunks:
        pick_whole(u_cat, 0, 0, u_pick, c)
    cut_items()
    build_chooser(0, 0, 0, folded[1:])
    sum_parts(0, lambda c: pick_whole(v_cat, 0, 1, v_pick, c))
    pl.semaphore_wait(barrier, len(met))
    send_parts(0)
    hold_places(GROUPS, spans)
    loads[3].wait()
    for r in range(spans):
        held[:, 2 * spans + r, :] = vals[0, :, r * LANES : (r + 1) * LANES]
    tiles[0] = held[0]
    for s in range(1, strata):
        tile_copy(s).start()

    @pl.loop(0, strata)
    def _(s):
        @pl.loop(0, per_tile - 1)
        def _(q):
            slot = (s * per_tile + q) % 2
            build_chooser(1 - slot, s, q + 1)
            for c in chunks:
                pick_whole(u_cat, 1 - slot, 0, u_pick, c)
                pick_whole(v_cat, 1 - slot, 1, v_pick, c)
            build_spreader(s, q)
            get_errors(s, q, slot)
            make_steps(slot, 1, v_step, (0,))
            make_steps(slot, 0, u_step, (0,))
            for t in range(0, item_keys, CHUNK):
                turn_part(v_step, user_keys, t, v_moved, v_turn)
            for t in range(0, user_keys, CHUNK):
                turn_part(u_step, 0, t, u_moved, u_turn)
            for c in chunks:
                pick_moved(v_turn, 1 - slot, 1, v_pick, c)
            sum_parts(1 - slot, lambda c: pick_moved(u_turn, 1 - slot, 0, u_pick, c))
            send_parts(1 - slot)
            make_steps(slot, 0, u_step, (1,))
            make_steps(slot, 1, v_step, (1,))
            for t in range(0, user_keys, CHUNK):
                add_users(s, t, u_moved[:, t : t + CHUNK] + spread(u_step[lows], t))
            for t in range(0, user_count, CHUNK):
                cut_users(s, t)
            for t in range(0, item_keys, CHUNK):
                add_items(t, v_moved[:, t : t + CHUNK] + spread(v_step[lows], user_keys + t))
            cut_items()
            for o in range(1, ranks):
                part_copy(slot, o).wait_send()

        q = per_tile - 1
        slot = (s * per_tile + q) % 2
        build_spreader(s, q)

        @pl.when(s < strata - 1)
        def _():
            tile_copy(s + 1).wait_recv()
            build_chooser(1 - slot, s + 1, 0)

        get_errors(s, q, slot)
        make_steps(slot, 0, u_step)
        for t in range(0, user_keys, CHUNK):
            add_users(s, t, spread_both(u_step, t))
        for t in range(0, user_count, CHUNK):
            user_copy(s, t).start()
        make_steps(slot, 1, v_step)
        for t in range(0, item_keys, CHUNK):
            add_items(t, spread_both(v_step, user_keys + t))
        for o in range(1, ranks):
            part_copy(slot, o).wait_send()

        @pl.when(s < strata - 1)
        def _():
            cut_items()
            for c in chunks:
                pick_whole(v_cat, 1 - slot, 1, v_pick, c)
            user_copy(s, 0).wait()
            cut_users(s + 1, 0)
            for c in chunks:
                here = slice(c, c + CHUNK)
                u_pick[1 - slot, :, here] = pick_half(0, c)
            for t in range(CHUNK, user_count, CHUNK):
                user_copy(s, t).wait()
                cut_users(s + 1, t)

            def pick_rest(c):
                second = pick_half(1, c)
                for g in range(0, CHUNK, LANES):
                    here = slice(c + g, c + g + LANES)
                    side = side_of(1 - slot, 0, (c + g) // LANES) > 0.5
                    u_pick[1 - slot, :, here] = jnp.where(
                        side, second[:, g : g + LANES], u_pick[1 - slot, :, here]
                    )

            sum_parts(1 - slot, pick_rest)
            send_parts(1 - slot)

    for s in range(1, strata):
        tile_copy(s).wait_send()
    for t in range(0, user_count, CHUNK):
        user_copy(strata - 1, t).wait()
        u_out[:, t : t + CHUNK] = users[strata, :, t : t + CHUNK]


def hand_over(u_in, v_in, u_out, v_out, sem):
    copies = [
        pltpu.make_async_copy(source, target, sem.at[i])
        for i, (source, target) in enumerate(((v_in, v_out), (u_in, u_out)))
    ]
    for copy in copies:
        copy.start()
    for copy in copies:
        copy.wait()


def solution(mesh):
    blocks, ranks = mesh.shape["blk"], mesh.shape["rank"]

    def per_device(user_factors, item_factors, tile_rows, tile_cols, tile_vals, tile_count):
        depth, user_count = user_factors.shape
        item_count = item_factors.shape[1]
        strata, tile = tile_rows.shape[1:]
        held = (strata, 3 * tile // LANES, LANES)
        vmem = pl.BlockSpec(memory_space=pltpu.VMEM)
        f32, bf16 = jnp.float32, jnp.bfloat16
        moved = pl.pallas_call(
            functools.partial(kernel, blocks, ranks),
            out_shape=(
                pltpu.VMEM((depth, user_count), f32),
                pltpu.VMEM((depth, item_count), f32),
            ),
            in_specs=[pl.BlockSpec(memory_space=pl.ANY)] * 6,
            out_specs=(vmem, vmem),
            scratch_shapes=[
                pltpu.VMEM(tile_rows.shape, jnp.int32),
                pltpu.VMEM(tile_cols.shape, jnp.int32),
                pltpu.VMEM(tile_vals.shape, f32),
                pltpu.SMEM(tile_count.shape, jnp.int32),
                pltpu.VMEM((strata + 1, depth, user_count), f32),
                pltpu.VMEM((2 * FOLD * depth, user_count // FOLD), bf16),
                pltpu.VMEM((2 * FOLD * depth, item_count // FOLD), bf16),
                pltpu.VMEM(held, f32),
                pltpu.VMEM(held, f32),
                pltpu.VMEM(((user_count + item_count) // FOLD, BATCH), bf16),
                pltpu.VMEM((2, 2, GROUPS, LANES), f32),
                pltpu.VMEM((BATCH, (user_count + item_count) // FOLD), bf16),
                pltpu.VMEM((2, depth, BATCH), f32),
                pltpu.VMEM((2, depth, BATCH), f32),
                pltpu.VMEM((2 * FOLD * depth, BATCH), bf16),
                pltpu.VMEM((2 * FOLD * depth, BATCH), bf16),
                pltpu.VMEM((FOLD * depth, user_count // FOLD), bf16),
                pltpu.VMEM((FOLD * depth, item_count // FOLD), bf16),
                pltpu.VMEM((FOLD * depth, user_count // FOLD), f32),
                pltpu.VMEM((FOLD * depth, item_count // FOLD), f32),
                pltpu.VMEM((2, GROUPS, LANES), f32),
                pltpu.VMEM((2, ranks - 1, GROUPS, LANES), f32),
                pltpu.VMEM((GROUPS, LANES), f32),
                pltpu.SemaphoreType.DMA((2, ranks - 1)),
                pltpu.SemaphoreType.DMA((2, ranks - 1)),
                pltpu.SemaphoreType.DMA((strata,)),
                pltpu.SemaphoreType.DMA((strata,)),
                pltpu.SemaphoreType.DMA((strata, user_count // CHUNK)),
                pltpu.SemaphoreType.DMA((strata, user_count // CHUNK)),
                pltpu.SemaphoreType.DMA((6,)),
            ],
            compiler_params=pltpu.CompilerParams(
                collective_id=0, has_side_effects=True, vmem_limit_bytes=60 * 1024 * 1024
            ),
        )(user_factors, item_factors, tile_rows, tile_cols, tile_vals, tile_count)
        return pl.pallas_call(
            hand_over,
            out_shape=(
                jax.ShapeDtypeStruct((depth, user_count), f32),
                jax.ShapeDtypeStruct((depth, item_count), f32),
            ),
            in_specs=[vmem, vmem],
            out_specs=[pl.BlockSpec(memory_space=pl.ANY)] * 2,
            scratch_shapes=[pltpu.SemaphoreType.DMA((2,))],
        )(*[pltpu.with_memory_space_constraint(x, pltpu.VMEM) for x in moved])

    placed = (
        P("rank", "blk"),
        P("rank", "blk"),
        P("blk", None, None),
        P("blk", None, None),
        P("blk", None, None),
        P("blk", None),
    )
    return jax.shard_map(
        per_device,
        mesh=mesh,
        in_specs=placed,
        out_specs=(P("rank", "blk"), P("rank", "blk")),
        check_vma=False,
    )
```
